32 devices in a mesh: fsdp: 4 (over y, x), ctx: 8 (over z, core).
Axes of the slice: x: 2, y: 2, z: 4, core: 2. Of those that a mesh axis runs over, the one named last changes fastest.
Arguments:
- inputs: bfloat16 [4, 2048, 768], P('fsdp', 'ctx'), may hold values from -6 to 6
- positions: int32 [4, 2048], P('fsdp', 'ctx'), may hold values from 0 to 2047, as said below
- in_weight: bfloat16 [768, 2304], P('fsdp'), may hold values from -0.21875 to 0.21875
- in_bias: bfloat16 [2304], P('fsdp'), may hold values from -0.3125 to 0.3125
- out_weight: bfloat16 [768, 768], P('fsdp'), may hold values from -0.109375 to 0.109375
- out_bias: bfloat16 [768], P('fsdp'), may hold values from -4 to 4
- up_weight: bfloat16 [768, 3072], P('fsdp'), may hold values from -0.21875 to 0.21875
- up_bias: bfloat16 [3072], P('fsdp'), may hold values from -6 to 6
- down_weight: bfloat16 [3072, 768], P('fsdp'), may hold values from -0.109375 to 0.109375
- down_bias: bfloat16 [768], P('fsdp'), may hold values from -4 to 4
- first_gain: bfloat16 [768], P('fsdp'), may hold values from 0.25 to 1.75
- first_shift: bfloat16 [768], P('fsdp'), may hold values from -4 to 4
- second_gain: bfloat16 [768], P('fsdp'), may hold values from 0.25 to 1.75
- second_shift: bfloat16 [768], P('fsdp'), may hold values from -4 to 4
- out_grad: bfloat16 [4, 2048, 768], P('fsdp', 'ctx'), may hold values from -6 to 6
Outputs:
- output: bfloat16 [4, 2048, 768], P('fsdp', 'ctx')
- input_gradient: float32 [4, 2048, 768], P('fsdp', 'ctx')
- in_weight_gradient: float32 [768, 2304], P('fsdp')
- in_bias_gradient: float32 [2304], P('fsdp')
- out_weight_gradient: float32 [768, 768], P('fsdp')
- out_bias_gradient: float32 [768], P('fsdp')
- up_weight_gradient: float32 [768, 3072], P('fsdp')
- up_bias_gradient: float32 [3072], P('fsdp')
- down_weight_gradient: float32 [3072, 768], P('fsdp')
- down_bias_gradient: float32 [768], P('fsdp')
- first_gain_gradient: float32 [768], P('fsdp')
- first_shift_gradient: float32 [768], P('fsdp')
- second_gain_gradient: float32 [768], P('fsdp')
- second_shift_gradient: float32 [768], P('fsdp')
The draws below stay inside these ranges and needn't reach their ends.
Inputs may be any that keep to these rules, and one draw needn't show every extreme that they name: Each row holds every position of its sequence once, in runs of 128 consecutive rising positions that start at multiples of 128; the order of the runs differs from row to row.
All inputs are finite; a program needn't handle non-finite values.
Results may differ from the reference program's by a relative error of at most 0.018.
Values may be sent and summed in bfloat16 or wider, within the bound.
No kernel may reach another device: no remote copies, remote signals or barrier semaphores. Data moves between devices by JAX's collectives and lax.ppermute only.
A program may use at most 192 MiB of HBM per device.

```python
import math
import jax
import jax.numpy as jnp
from jax import lax

D = 768
HEADS = 12
HEAD = 64
ROT = 16
FF = 3072
SEQS = 4
LENGTH = 2048
PIECE = 128
PIECES = 16


def draw_positions(key, part):
    key = jax.random.fold_in(key, 7)
    row_keys = jax.random.split(key, SEQS)

    def one_row(row_key):
        order = jax.random.permutation(row_key, PIECES)
        return (order[:, None] * PIECE + jnp.arange(PIECE)[None, :]).reshape(LENGTH)
    return jax.vmap(one_row)(row_keys).astype(jnp.int32)


def shard_levels(key, extent, shards, smallest, high):
    factor_of = 1.0
    for axis_at, shards_of in shards:
        draws = jax.random.uniform(jax.random.fold_in(jax.random.fold_in(key, 6), axis_at), (shards_of,), jnp.float32, smallest / len(shards), high / len(shards))
        factor_of = factor_of * jnp.repeat(jnp.exp(draws), extent[axis_at] // shards_of).reshape((-1,) + (1,) * (len(extent) - 1 - axis_at))
    return factor_of


def gaussian(own_key, dims, scale, limit, cuts=(), held_as=jnp.bfloat16):
    values = scale * jax.random.normal(own_key, dims, jnp.float32)
    if cuts:
        values = values * shard_levels(own_key, dims, cuts, -0.22, 0.18)
    return jnp.clip(values, -limit, limit).astype(held_as)


def setup_inputs(seed: int = 0) -> dict:
    seeds = jax.random.split(jax.random.key(seed), 16)
    inputs = gaussian(seeds[0], (SEQS, LENGTH, D), 1.0, 6.0, ((0, 4), (1, 8)))
    positions = draw_positions(jax.random.fold_in(seeds[15], 71), 0)
    in_weight = gaussian(seeds[2], (D, 3 * D), D ** -0.5, 0.21875, ((0, 4),))
    in_bias = gaussian(seeds[3], (3 * D,), 0.02, 0.3125, ((0, 4),))
    out_weight = gaussian(seeds[4], (D, D), (max(1, 10 * D * D // LENGTH)) ** -0.5, 0.109375, ((0, 4),))
    out_bias = gaussian(seeds[5], (D,), 0.3, 4.0, ((0, 4),))
    up_weight = gaussian(seeds[6], (D, FF), D ** -0.5, 0.21875, ((0, 4),))
    up_bias = gaussian(seeds[7], (FF,), 0.5, 6.0, ((0, 4),))
    down_weight = gaussian(seeds[8], (FF, D), FF ** -0.5, 0.109375, ((0, 4),))
    down_bias = gaussian(seeds[9], (D,), 0.3, 4.0, ((0, 4),))
    first_gain = jnp.clip(1.0 + 0.15 * jax.random.normal(seeds[10], (D,), jnp.float32), 0.25, 1.75).astype(jnp.bfloat16)
    first_shift = gaussian(seeds[11], (D,), 0.3, 4.0, ((0, 4),))
    second_gain = jnp.clip(1.0 + 0.15 * jax.random.normal(seeds[12], (D,), jnp.float32), 0.25, 1.75).astype(jnp.bfloat16)
    second_shift = gaussian(seeds[13], (D,), 0.3, 4.0, ((0, 4),))
    out_grad = gaussian(seeds[14], (SEQS, LENGTH, D), 1.0, 6.0, ((0, 4), (1, 8)))
    return dict(inputs=inputs, positions=positions, in_weight=in_weight, in_bias=in_bias, out_weight=out_weight, out_bias=out_bias, up_weight=up_weight, up_bias=up_bias, down_weight=down_weight, down_bias=down_bias, first_gain=first_gain, first_shift=first_shift, second_gain=second_gain, second_shift=second_shift, out_grad=out_grad)


@jax.custom_vjp
def low(v):
    return lax.optimization_barrier(v.astype(jnp.bfloat16)).astype(jnp.float32)

@jax.custom_vjp
def low_back(v):
    return v

def low_keep(v):
    return (low(v), None)

def low_pass(kept, grad):
    return (grad,)

def back_keep(v):
    return (v, None)

def back_low(kept, grad):
    return (low(grad),)
low.defvjp(low_keep, low_pass)
low_back.defvjp(back_keep, back_low)
NEG = -1e+30
EPS = 1e-05
HIGH = lax.Precision.HIGHEST

def layer_norm(values, gain, shift):
    mean = lax.optimization_barrier(jnp.mean(values, -1, keepdims=True))
    centred = values - mean
    spread = lax.optimization_barrier(jnp.mean(centred * centred, -1, keepdims=True))
    return centred * lax.rsqrt(spread + EPS) * gain + shift

def turn_tables(positions):
    ladder = 10000.0 ** (-jnp.arange(0, ROT, 2, dtype=jnp.float32) / ROT)
    angle = positions.astype(jnp.float32)[..., None] * ladder
    angle = jnp.concatenate([angle, angle], -1)
    return (jnp.cos(angle), jnp.sin(angle))

def rotate(values, cosine, sine):
    half = ROT // 2
    part = values[..., :ROT]
    turned = jnp.concatenate([-part[..., half:], part[..., :half]], -1)
    part = part * cosine[..., None, :] + turned * sine[..., None, :]
    return jnp.concatenate([part, values[..., ROT:]], -1)

def attend_block(queries, query_pos, keys, values, key_pos):
    scores = jnp.einsum('qhd,khd->hqk', queries, keys, precision=HIGH) * (1.0 / math.sqrt(HEAD))
    scores = low_back(scores)
    allowed = (key_pos[None, :] <= query_pos[:, None])[None]
    scores = jnp.where(allowed, scores, NEG)
    peak = lax.optimization_barrier(jnp.max(scores, -1, keepdims=True))
    raised = jnp.exp(scores - peak)
    probs = low(raised / lax.optimization_barrier(jnp.sum(raised, -1, keepdims=True)))
    return jnp.einsum('hqk,khd->qhd', probs, values, precision=HIGH)

def sequence_attention(queries, keys, values, positions):
    length = queries.shape[0]
    size = 512 if length % 512 == 0 else length
    blocks = length // size
    query_blocks = queries.reshape(blocks, size, HEADS, HEAD)
    place_blocks = positions.reshape(blocks, size)
    stepper = jax.checkpoint(attend_block)
    result = lax.map(lambda group: stepper(group[0], group[1], keys, values, positions), (query_blocks, place_blocks))
    return result.reshape(length, HEADS, HEAD)

def forward(inputs, positions, in_weight, in_bias, out_weight, out_bias, up_weight, up_bias, down_weight, down_bias, first_gain, first_shift, second_gain, second_shift):
    seqs, length, width = inputs.shape
    flat = inputs.reshape(seqs * length, width)
    first = low(layer_norm(flat, first_gain, first_shift))
    second = low(layer_norm(flat, second_gain, second_shift))
    projected = low_back(jnp.dot(first, in_weight, precision=HIGH) + in_bias)
    projected = projected.reshape(seqs, length, 3, HEADS, HEAD)
    cosine, sine = turn_tables(positions)
    queries = low(rotate(projected[:, :, 0], cosine, sine))
    keys = low(rotate(projected[:, :, 1], cosine, sine))
    values = low(projected[:, :, 2])
    attended = lax.map(lambda group: sequence_attention(*group), (queries, keys, values, positions))
    mixed = low(low_back(attended)).reshape(seqs * length, width)
    up = low_back(jnp.dot(second, up_weight, precision=HIGH) + up_bias)
    activated = low(jax.nn.gelu(up, approximate=False))
    branch_attn = jnp.dot(mixed, out_weight, precision=HIGH) + out_bias
    branch_ff = jnp.dot(activated, down_weight, precision=HIGH) + down_bias
    return (flat + branch_attn + branch_ff).reshape(seqs, length, width)

def reference(inputs, positions, in_weight, in_bias, out_weight, out_bias, up_weight, up_bias, down_weight, down_bias, first_gain, first_shift, second_gain, second_shift, out_grad):
    params = [a.astype(jnp.float32) for a in (in_weight, in_bias, out_weight, out_bias, up_weight, up_bias, down_weight, down_bias, first_gain, first_shift, second_gain, second_shift)]

    def apply(values, *weights):
        return forward(values, positions, *weights)
    output, pullback = jax.vjp(apply, inputs.astype(jnp.float32), *params)
    grads = pullback(out_grad.astype(jnp.float32))
    return (output.astype(jnp.bfloat16), grads[0], grads[1], grads[2], grads[3], grads[4], grads[5], grads[6], grads[7], grads[8], grads[9], grads[10], grads[11], grads[12])
```

```python
import functools
import math

import jax
import jax.numpy as jnp
from jax import lax
from jax.experimental import pallas as pl
from jax.experimental.pallas import tpu as pltpu
from jax.sharding import PartitionSpec as P

HEAD = 64
ROT = 16
HALF = ROT // 2
RUN = 128
TILE = 256
NEG = -1e30
EPS = 1e-05
BF = jnp.bfloat16
F32 = jnp.float32
VMEM_LIMIT = 60 * 1024 * 1024


def mm(left, right, dims):
    return lax.dot_general(left, right, ((dims[:1], dims[1:]), ((), ())), preferred_element_type=F32)


def flip(x):
    return x.astype(F32).T.astype(x.dtype)


def normalize(values):
    mean = jnp.mean(values, -1, keepdims=True)
    centred = values - mean
    spread = jnp.mean(centred * centred, -1, keepdims=True)
    inverse = lax.rsqrt(spread + EPS)
    return centred * inverse, inverse


def turn(values, cosine, sine):
    one, two = values[:HALF], values[HALF:ROT]
    return jnp.concatenate([one * cosine - two * sine, two * cosine + one * sine, values[ROT:]], 0)


def ff_kernel(x_ref, g_ref, up_ref, down_ref, upb_ref, gain_ref, shift_ref,
              out_ref, back_ref, dup_ref, ddown_ref, dbias_ref, dgain_ref, dshift_ref,
              acc_up, acc_down):
    step = pl.program_id(0)

    @pl.when(step == 0)
    def _():
        acc_up[...] = jnp.zeros_like(acc_up)
        acc_down[...] = jnp.zeros_like(acc_down)
        dbias_ref[...] = jnp.zeros_like(dbias_ref)
        dgain_ref[...] = jnp.zeros_like(dgain_ref)
        dshift_ref[...] = jnp.zeros_like(dshift_ref)

    xhat, _ = normalize(x_ref[0].astype(F32))
    second = (xhat * gain_ref[...] + shift_ref[...]).astype(BF)
    up = mm(second, up_ref[...], (1, 0)) + upb_ref[...]
    phi = 0.5 * (1.0 + lax.erf(up * (1.0 / math.sqrt(2.0))))
    active = (up * phi).astype(BF)
    slope = phi + up * jnp.exp(-0.5 * up * up) * (1.0 / math.sqrt(2.0 * math.pi))
    out_ref[0] = mm(active, down_ref[...], (1, 0)).astype(BF)
    grad = g_ref[0]
    back_up = mm(grad, down_ref[...], (1, 1)) * slope
    low_up = back_up.astype(BF)
    dbias_ref[...] += jnp.sum(low_up.astype(F32), 0, keepdims=True)
    acc_up[...] += mm(second, low_up, (0, 0))
    acc_down[...] += mm(active, grad, (0, 0))
    back = mm(low_up, up_ref[...], (1, 1))
    dgain_ref[...] += jnp.sum(back * xhat, 0, keepdims=True)
    dshift_ref[...] += jnp.sum(back, 0, keepdims=True)
    back_ref[0] = (back * gain_ref[...]).astype(BF)

    @pl.when(step == pl.num_programs(0) - 1)
    def _():
        dup_ref[...] = acc_up[...].astype(BF)
        ddown_ref[...] = acc_down[...].astype(BF)


def whole(shape):
    return pl.BlockSpec(shape, lambda *_: (0,) * len(shape))


def feed_forward(x, grad, up, down, up_bias, gain, shift):
    groups, tokens, width = x.shape
    hidden = up.shape[1]
    tile = pl.BlockSpec((1, tokens, width), lambda i: (i, 0, 0))
    row = jax.ShapeDtypeStruct((1, width), F32)
    return pl.pallas_call(
        ff_kernel,
        grid=(groups,),
        in_specs=[tile, tile, whole((width, hidden)), whole((hidden, width)), whole((1, hidden)),
                  whole((1, width)), whole((1, width))],
        out_specs=[tile, tile, whole((width, hidden)), whole((hidden, width)), whole((1, hidden)),
                   whole((1, width)), whole((1, width))],
        out_shape=[jax.ShapeDtypeStruct(x.shape, BF), jax.ShapeDtypeStruct(x.shape, BF),
                   jax.ShapeDtypeStruct((width, hidden), BF), jax.ShapeDtypeStruct((hidden, width), BF),
                   jax.ShapeDtypeStruct((1, hidden), F32), row, row],
        scratch_shapes=[pltpu.VMEM((width, hidden), F32), pltpu.VMEM((hidden, width), F32)],
        compiler_params=pltpu.CompilerParams(vmem_limit_bytes=VMEM_LIMIT),
        name="feed_forward",
    )(x, grad, up, down, up_bias, gain, shift)


def qkv_kernel(order_ref, xa_ref, xb_ref, w_ref, bias_ref, gain_ref, shift_ref, cos_ref, sin_ref, out_ref):
    values = jnp.concatenate([xa_ref[0], xb_ref[0]], 0).astype(F32)
    xhat, _ = normalize(values)
    first = (xhat * gain_ref[...] + shift_ref[...]).astype(BF)
    proj = mm(w_ref[...], first, (1, 1)) + bias_ref[...]
    heads = out_ref.shape[0] // 3
    cosine, sine = cos_ref[0], sin_ref[0]
    for i in range(3 * heads):
        part = proj[i * HEAD:(i + 1) * HEAD]
        if i < 2 * heads:
            part = turn(part, cosine, sine)
        part = part.astype(BF)
        if i < heads:
            part = part * jnp.asarray(1.0 / math.sqrt(HEAD), BF)
        out_ref[i, 0] = part


def run_specs(width):
    return [pl.BlockSpec((1, RUN, width), lambda i, order, k=k: (order[2 * i + k], 0, 0)) for k in (0, 1)]


def project(order, x, w, bias, gain, shift, cosine, sine):
    runs, _, width = x.shape
    rows = w.shape[0]
    tiles = runs // 2
    parts = rows // HEAD
    table = pl.BlockSpec((1, HALF, TILE), lambda i, order: (i, 0, 0))
    return pl.pallas_call(
        qkv_kernel,
        grid_spec=pltpu.PrefetchScalarGridSpec(
            num_scalar_prefetch=1,
            grid=(tiles,),
            in_specs=run_specs(width) + [whole((rows, width)), whole((rows, 1)), whole((1, width)),
                                         whole((1, width)), table, table],
            out_specs=pl.BlockSpec((parts, 1, HEAD, TILE), lambda i, order: (0, i, 0, 0)),
        ),
        out_shape=jax.ShapeDtypeStruct((parts, tiles, HEAD, TILE), BF),
        compiler_params=pltpu.CompilerParams(vmem_limit_bytes=VMEM_LIMIT),
        name="project",
    )(order, x, x, w, bias, gain, shift, cosine, sine)


def attention_kernel(share, place_ref, q_ref, k_ref, v_ref, da_ref, db_ref, cos_ref, sin_ref,
                     mix_ref, back_ref, keys, values, dkeys, dvalues, sbuf, pbuf):
    head, step = pl.program_id(0), pl.program_id(1)
    heads, steps = pl.num_programs(0), pl.num_programs(1)
    tiles = k_ref.shape[1]
    block = share(step, place_ref)

    @pl.when((head == 0) & (step == 0))
    def _():
        mix_ref[...] = jnp.zeros_like(mix_ref)
        back_ref[...] = jnp.zeros_like(back_ref)

    @pl.when(step == 0)
    def _():
        @pl.loop(0, tiles)
        def _(j):
            keys[j] = flip(k_ref[0, j])
            values[j] = flip(v_ref[0, j])
            dkeys[j] = jnp.zeros((TILE, HEAD), F32)
            dvalues[j] = jnp.zeros((TILE, HEAD), F32)

    query = q_ref[0, 0]

    def fold(x, op):
        return op(x.reshape(TILE // 8, 8, TILE), 0)

    def score(j, peak):
        s = mm(keys[j], query, (1, 0))
        sbuf[j] = s
        return jnp.maximum(peak, fold(s, jnp.max))

    peak = lax.fori_loop(0, block, score, jnp.full((8, TILE), NEG, F32))
    s = mm(keys[block], query, (1, 0))
    key_at = lax.broadcasted_iota(jnp.int32, (TILE, TILE), 0)
    query_at = lax.broadcasted_iota(jnp.int32, (TILE, TILE), 1)
    s = jnp.where(key_at <= query_at, s, NEG)
    sbuf[block] = s
    peak = jnp.maximum(peak, fold(s, jnp.max))
    peak = jnp.max(peak, 0, keepdims=True)

    def weigh(j, carry):
        total, mixed = carry
        p = jnp.exp(sbuf[j] - peak)
        low = p.astype(BF)
        pbuf[j] = low
        return total + fold(p, jnp.sum), mixed + mm(v_ref[0, j], low, (1, 0))

    total, mixed = lax.fori_loop(
        0, block + 1, weigh, (jnp.zeros((8, TILE), F32), jnp.zeros((HEAD, TILE), F32)))
    inverse = 1.0 / jnp.sum(total, 0, keepdims=True)
    mixed = mixed * inverse
    low_mixed = mixed.astype(BF)
    for k in (0, 1):
        at = place_ref[1 + 2 * block + k]
        mix_ref[at // 2, head, at % 2] = low_mixed[:, k * RUN:(k + 1) * RUN]
    back = jnp.concatenate([da_ref[0], db_ref[0]], 1).astype(F32) * inverse
    spread = jnp.sum(back * mixed, 0, keepdims=True)
    back = back.astype(BF)
    back_rows = flip(back)
    query_rows = flip(query)

    def pull(j, dquery):
        low = pbuf[j]
        dp = mm(values[j], back, (1, 0))
        ds = (low.astype(F32) * (dp - spread)).astype(BF)
        dvalues[j] += mm(low, back_rows, (1, 0))
        dkeys[j] += mm(ds, query_rows, (1, 0))
        return dquery + mm(k_ref[0, j], ds, (1, 0))

    dquery = lax.fori_loop(0, block + 1, pull, jnp.zeros((HEAD, TILE), F32))
    dquery = dquery * (1.0 / math.sqrt(HEAD))
    back_ref[head, block] = turn(dquery, cos_ref[block], -sin_ref[block]).astype(BF)

    @pl.when(step == steps - 1)
    def _():
        @pl.loop(0, tiles)
        def _(j):
            back_ref[heads + head, j] = turn(dkeys[j].T, cos_ref[j], -sin_ref[j]).astype(BF)
            back_ref[2 * heads + head, j] = dvalues[j].T.astype(BF)


def attend(place, qkv, back, cosine, sine, sharers):
    parts, tiles, _, _ = qkv.shape
    heads = parts // 3
    owners = back.shape[0]
    steps = tiles // sharers

    def share(step, place_ref):
        return 2 * sharers * (step // 2) + jnp.where(step % 2 == 0, place_ref[0], 2 * sharers - 1 - place_ref[0])

    def run_of(h, n, place_ref, k):
        at = place_ref[1 + 2 * share(n, place_ref) + k]
        return at // 2, h, at % 2

    all_tiles = (1, tiles, HEAD, TILE)
    return pl.pallas_call(
        functools.partial(attention_kernel, share),
        grid_spec=pltpu.PrefetchScalarGridSpec(
            num_scalar_prefetch=1,
            grid=(heads, steps),
            in_specs=[
                pl.BlockSpec((1, 1, HEAD, TILE), lambda h, n, p: (h, share(n, p), 0, 0)),
                pl.BlockSpec(all_tiles, lambda h, n, p: (heads + h, 0, 0, 0)),
                pl.BlockSpec(all_tiles, lambda h, n, p: (2 * heads + h, 0, 0, 0)),
                pl.BlockSpec((1, HEAD, RUN), lambda h, n, p: run_of(h, n, p, 0)),
                pl.BlockSpec((1, HEAD, RUN), lambda h, n, p: run_of(h, n, p, 1)),
                whole((tiles, HALF, TILE)),
                whole((tiles, HALF, TILE)),
            ],
            out_specs=[whole((owners, heads, 2, HEAD, RUN)), whole((parts, tiles, HEAD, TILE))],
            scratch_shapes=[
                pltpu.VMEM((tiles, TILE, HEAD), BF),
                pltpu.VMEM((tiles, TILE, HEAD), BF),
                pltpu.VMEM((tiles, TILE, HEAD), F32),
                pltpu.VMEM((tiles, TILE, HEAD), F32),
                pltpu.VMEM((tiles, TILE, TILE), F32),
                pltpu.VMEM((tiles, TILE, TILE), BF),
            ],
        ),
        out_shape=[jax.ShapeDtypeStruct((owners, heads, 2, HEAD, RUN), BF),
                   jax.ShapeDtypeStruct((parts, tiles, HEAD, TILE), BF)],
        compiler_params=pltpu.CompilerParams(vmem_limit_bytes=VMEM_LIMIT),
        name="attend",
    )(place, qkv, qkv, qkv, back, back, cosine, sine)


def back_kernel(order_ref, b_ref, w_ref, xa_ref, xb_ref, gain_ref, shift_ref,
                e_ref, dw_ref, dbias_ref, dgain_ref, dshift_ref, acc):
    step = pl.program_id(0)

    @pl.when(step == 0)
    def _():
        acc[...] = jnp.zeros_like(acc)
        dbias_ref[...] = jnp.zeros_like(dbias_ref)
        dgain_ref[...] = jnp.zeros_like(dgain_ref)
        dshift_ref[...] = jnp.zeros_like(dshift_ref)

    values = jnp.concatenate([xa_ref[0], xb_ref[0]], 0).astype(F32)
    xhat, _ = normalize(values)
    first = (xhat * gain_ref[...] + shift_ref[...]).astype(BF)
    rows = b_ref.shape[0] * HEAD
    back = b_ref[...].reshape(rows, TILE)
    acc[...] += mm(back, first, (1, 0))
    dbias_ref[...] += jnp.sum(back.astype(F32), 1, keepdims=True)
    e = mm(back, w_ref[...], (0, 0))
    dgain_ref[...] += jnp.sum(e * xhat, 0, keepdims=True)
    dshift_ref[...] += jnp.sum(e, 0, keepdims=True)
    e = (e * gain_ref[...]).astype(BF)
    e_ref[order_ref[2 * step]] = e[:RUN]
    e_ref[order_ref[2 * step + 1]] = e[RUN:]

    @pl.when(step == pl.num_programs(0) - 1)
    def _():
        dw_ref[...] = acc[...].T.astype(BF)


def project_back(order, back, w, x, gain, shift):
    runs, _, width = x.shape
    rows = w.shape[0]
    parts, tiles, _, _ = back.shape
    line = jax.ShapeDtypeStruct((1, width), F32)
    return pl.pallas_call(
        back_kernel,
        grid_spec=pltpu.PrefetchScalarGridSpec(
            num_scalar_prefetch=1,
            grid=(tiles,),
            in_specs=[pl.BlockSpec((parts, 1, HEAD, TILE), lambda i, order: (0, i, 0, 0)), whole((rows, width))]
            + run_specs(width) + [whole((1, width)), whole((1, width))],
            out_specs=[whole((runs, RUN, width)), whole((width, rows)), whole((rows, 1)), whole((1, width)),
                       whole((1, width))],
            scratch_shapes=[pltpu.VMEM((rows, width), F32)],
        ),
        out_shape=[jax.ShapeDtypeStruct((runs, RUN, width), BF), jax.ShapeDtypeStruct((width, rows), BF),
                   jax.ShapeDtypeStruct((rows, 1), F32), line, line],
        compiler_params=pltpu.CompilerParams(vmem_limit_bytes=VMEM_LIMIT),
        name="project_back",
    )(order, back, w, x, x, gain, shift)


def spread_out(pieces, axis, groups=None):
    return lax.all_to_all(pieces, axis, 0, 0, axis_index_groups=groups)


def to_all(x, axis, groups=None, count=None):
    count = count or lax.axis_size(axis)
    return spread_out(jnp.broadcast_to(x[None], (count,) + x.shape), axis, groups)


def on_device(
    inputs, positions, in_weight, in_bias, out_weight, out_bias, up_weight, up_bias, down_weight, down_bias,
    first_gain, first_shift, second_gain, second_shift, out_grad,
):
    x, grad, place = inputs[0], out_grad[0], positions[0]
    tokens, width = x.shape
    owners, shards = lax.axis_size("ctx"), lax.axis_size("fsdp")
    here, shard = lax.axis_index("ctx"), lax.axis_index("fsdp")
    heads = width // HEAD
    groups = math.gcd(heads, owners // 2)
    sharers = owners // groups
    own_heads = heads // groups
    cols = own_heads * HEAD
    group, sharer, core = here // sharers, here % sharers, here % 2
    hidden = down_weight.shape[0]
    rows = in_weight.shape[0]
    half = rows // 2
    length = tokens * owners
    tiles = length // TILE
    parity = [[i for i in range(owners) if i % 2 == k] for k in (0, 1)]
    pairs = [(i, i ^ 1) for i in range(owners)]

    def swap(value):
        return lax.ppermute(value, "ctx", pairs)

    def both(mine, other):
        return jnp.stack([jnp.where(core == 0, mine, other), jnp.where(core == 0, other, mine)], 1)

    x_all = lax.all_gather(x, "ctx", axis=0, tiled=True)

    smalls = [in_bias, out_bias, down_bias, first_gain, first_shift, second_gain, second_shift]
    sizes = [s.shape[0] for s in smalls]
    packed = jnp.concatenate(smalls)
    small_rows = -(-packed.shape[0] // hidden)
    packed = jnp.pad(packed, (0, small_rows * hidden - packed.shape[0])).reshape(small_rows, hidden)

    def own_half(value):
        return lax.dynamic_slice_in_dim(value, core * half, half, 0)

    up_pieces = own_half(up_weight).reshape(half, shards, hidden).transpose(1, 0, 2)
    packed = jnp.broadcast_to(packed[None], (shards, small_rows, hidden))
    up_got = spread_out(jnp.concatenate([up_pieces, packed], 1), "fsdp")
    x_plane = to_all(x, "fsdp")
    grad_plane = to_all(grad, "fsdp")
    in_own = own_half(in_weight).reshape(half, 3, groups, cols)
    in_own = lax.dynamic_index_in_dim(in_own, group, 2, keepdims=False).reshape(half, 3 * cols)
    in_own = jnp.pad(in_own, ((0, 0), (0, width - 3 * cols)))
    io_got = to_all(jnp.concatenate([own_half(out_weight), in_own], 0), "fsdp")

    up_own, small_got = up_got[:, :half], up_got[:, half:].reshape(shards, -1)
    up_full = both(up_own, swap(up_own)).reshape(width, hidden)
    small, at = [], 0
    for size in sizes:
        small.append(small_got[:, at:at + size].reshape(-1).astype(F32))
        at += size
    full_in_bias, full_out_bias, full_down_bias, gain_one, shift_one, gain_two, shift_two = small

    out_part, back_part, up_part, down_part, up_bias_part, gain_two_part, shift_two_part = feed_forward(
        x_plane, grad_plane, up_full, down_weight, up_bias.astype(F32)[None], gain_two[None], shift_two[None])
    ff_got = spread_out(jnp.concatenate([out_part, back_part], 1), "fsdp")
    ff_sum = jnp.sum(ff_got.astype(F32), 0)

    small_step = rows // owners
    up_pieces = up_part.reshape(shards, owners, small_step, hidden).transpose(1, 0, 2, 3)
    up_pieces = up_pieces.reshape(owners, shards * small_step, hidden)
    down_pieces = down_part.reshape(owners, hidden // owners, width)
    joined = hidden == width

    def joint(values, call):
        if not joined:
            return [call(v) for v in values]
        got = call(jnp.concatenate(values, -2))
        cut = values[0].shape[-2]
        return [got[..., :cut, :], got[..., cut:, :]]

    up_sum, down_sum = joint(
        [up_pieces, down_pieces], lambda v: lax.psum_scatter(v, "ctx", scatter_dimension=0, tiled=False))
    up_sum = spread_out(up_sum.reshape(shards, small_step, hidden), "fsdp").reshape(shards * small_step, hidden)

    def gather_owners(value):
        mine = to_all(value, "ctx", parity, owners // 2)
        return both(mine, swap(mine)).reshape((owners,) + value.shape)

    up_all, down_all = joint([up_sum, down_sum], gather_owners)
    up_weight_gradient = up_all.reshape(owners, shards, small_step, hidden).transpose(0, 2, 1, 3)
    up_weight_gradient = up_weight_gradient.reshape(rows, shards * hidden).astype(F32)
    down_weight_gradient = down_all.reshape(hidden, width).astype(F32)

    io_full = both(io_got, swap(io_got)).reshape(shards, 2, 2, half, width)
    out_full = io_full[:, :, 0].reshape(width, width)
    in_full = io_full[:, :, 1].reshape(width, width)[:, :3 * cols].T
    back_mixed = mm(out_full, grad, (1, 1)).astype(BF).reshape(groups, 1, cols, tokens)
    back_mixed = jnp.broadcast_to(back_mixed, (groups, sharers, cols, tokens)).reshape(owners, cols, tokens)
    run_rows = jnp.broadcast_to((place // RUN).astype(BF)[None, None], (owners, 8, tokens))
    back_got = spread_out(jnp.concatenate([back_mixed, run_rows], 1), "ctx")
    run_at = back_got[:, cols, ::RUN].reshape(-1).astype(jnp.int32)
    runs = run_at.shape[0]
    at_run = lax.broadcasted_iota(jnp.int32, (runs, runs), 0)
    of_run = lax.broadcasted_iota(jnp.int32, (runs, runs), 1)
    order = jnp.sum(jnp.where(run_at[None] == at_run, of_run, 0), 1)

    ladder = 10000.0 ** (-jnp.arange(0, ROT, 2, dtype=F32) / ROT)
    angle = jnp.arange(length, dtype=jnp.int32).astype(F32).reshape(tiles, 1, TILE) * ladder[None, :, None]
    cosine, sine = jnp.cos(angle), jnp.sin(angle)

    x_runs = x_all.reshape(runs, RUN, width)
    bias_own = lax.dynamic_index_in_dim(full_in_bias.reshape(3, groups, cols), group, 1, keepdims=False)
    qkv = project(order, x_runs, in_full, bias_own.reshape(-1, 1), gain_one[None], shift_one[None], cosine, sine)
    spots = jnp.concatenate([sharer[None].astype(jnp.int32), order])
    mixed_out, back_qkv = attend(spots, qkv, back_got, cosine, sine, sharers)
    e_runs, in_part, in_bias_part, gain_one_part, shift_one_part = project_back(
        order, back_qkv, in_full, x_runs, gain_one[None], shift_one[None])
    e_sum = lax.psum_scatter(e_runs.reshape(length, width), "ctx", scatter_dimension=0, tiled=True)

    mixed_got = spread_out(mixed_out, "ctx").astype(F32)
    mixed = jnp.sum(mixed_got.reshape(groups, sharers, own_heads, 2, HEAD, RUN), 1)
    mixed = mixed.transpose(0, 1, 3, 2, 4).reshape(width, tokens).astype(BF)
    branch = mm(mixed, out_full, (0, 0))
    out_part = mm(mixed, grad, (1, 0)).astype(BF)

    x32, grad32 = x.astype(F32), grad.astype(F32)
    output = x32 + (branch + full_out_bias) + (ff_sum[:tokens] + full_down_bias)

    in_bias_full = lax.dynamic_update_slice_in_dim(
        jnp.zeros((3, groups, cols), F32), in_bias_part.reshape(3, 1, cols), group, 1)
    lines = [in_bias_full.reshape(-1), jnp.sum(grad32, 0), gain_one_part[0], shift_one_part[0], gain_two_part[0],
             shift_two_part[0]]
    lines = [v.reshape(shards, -1) for v in lines]
    mine = (jnp.arange(shards) == shard)[:, None]
    lines.append(jnp.where(mine, up_bias_part, 0.0))
    line_sizes = [v.shape[1] for v in lines]
    lines = jnp.concatenate(lines, 1).astype(BF).reshape(shards, 2, -1, width - 3 * cols)
    line_rows = lines.shape[2]
    lines = jnp.pad(lines, ((0, 0), (0, 0), (0, half - line_rows), (0, 0)))
    in_pieces = jnp.concatenate([in_part.reshape(shards, 2, half, 3 * cols), lines], 3)
    pieces = jnp.concatenate([out_part.reshape(shards, 2, half, width), in_pieces], 2)
    keep = lax.dynamic_index_in_dim(pieces, core, 1, keepdims=False)
    give = lax.dynamic_index_in_dim(pieces, 1 - core, 1, keepdims=False)
    pieces = (keep.astype(F32) + swap(give).astype(F32)).astype(BF)
    pieces = jnp.sum(spread_out(pieces, "fsdp").astype(F32), 0).astype(BF)
    gathered = gather_owners(pieces).astype(F32).reshape(groups, sharers // 2, 2, 2, half, width)
    out_weight_gradient = jnp.sum(gathered[:, :, :, 0], (0, 1)).reshape(rows, width)
    in_sum = jnp.sum(gathered[:, :, :, 1], 1)
    in_weight_gradient = in_sum[..., :3 * cols].reshape(groups, rows, 3, cols).transpose(1, 2, 0, 3)
    in_weight_gradient = in_weight_gradient.reshape(rows, 3 * width)
    line_sum = jnp.sum(in_sum[:, :, :line_rows, 3 * cols:], 0).reshape(-1)
    totals, at = [], 0
    for size in line_sizes:
        totals.append(line_sum[at:at + size])
        at += size

    e = e_sum.astype(F32) + ff_sum[tokens:]
    xhat, inverse = normalize(x32)
    input_gradient = grad32 + inverse * (
        e - jnp.mean(e, -1, keepdims=True) - xhat * jnp.mean(e * xhat, -1, keepdims=True))
    return (
        output.astype(BF)[None], input_gradient[None], in_weight_gradient, totals[0], out_weight_gradient, totals[1],
        up_weight_gradient, totals[6], down_weight_gradient, totals[1], totals[2], totals[3], totals[4], totals[5],
    )


def solution(mesh):
    token, matrix, vector = P("fsdp", "ctx", None), P("fsdp", None), P("fsdp")
    return jax.shard_map(
        on_device,
        mesh=mesh,
        in_specs=(token, P("fsdp", "ctx"), matrix, vector, matrix, vector, matrix, vector, matrix, vector,
                  vector, vector, vector, vector, token),
        out_specs=(token, token, matrix, vector, matrix, vector, matrix, vector, matrix, vector,
                   vector, vector, vector, vector),
        check_vma=False,
    )
```

```python
import functools
import math

import jax
import jax.numpy as jnp
from jax import lax
from jax.experimental import pallas as pl
from jax.experimental.pallas import tpu as pltpu
from jax.sharding import PartitionSpec as P

HEAD = 64
ROT = 16
HALF = ROT // 2
RUN = 128
TILE = 256
NEG = -1e30
EPS = 1e-05
BF = jnp.bfloat16
F32 = jnp.float32
VMEM_LIMIT = 60 * 1024 * 1024


def mm(left, right, dims):
    return lax.dot_general(left, right, ((dims[:1], dims[1:]), ((), ())), preferred_element_type=F32)


def flip(x):
    return x.astype(F32).T.astype(x.dtype)


def normalize(values):
    mean = jnp.mean(values, -1, keepdims=True)
    centred = values - mean
    spread = jnp.mean(centred * centred, -1, keepdims=True)
    inverse = lax.rsqrt(spread + EPS)
    return centred * inverse, inverse


def turn(values, cosine, sine):
    one, two = values[:HALF], values[HALF:ROT]
    return jnp.concatenate([one * cosine - two * sine, two * cosine + one * sine, values[ROT:]], 0)


def ff_kernel(packed, core_ref, x_ref, g_ref, small_ref, mine_ref, mine_end_ref, other_ref, down_ref, upb_ref,
              *refs):
    shards = small_ref.shape[0]
    outs, refs = refs[:shards], refs[shards:]
    (dup_ref, ddown_ref, dbias_ref, dgain_ref, dshift_ref, acc_up, acc_down, up_ref, gain_ref, shift_ref) = refs
    step = pl.program_id(0)

    @pl.when(step == 0)
    def _():
        half = other_ref.shape[1]
        share = gain_ref.shape[1] // shards
        first = core_ref[0] == 0
        for f in range(shards):
            mine = jnp.concatenate([mine_ref[f].astype(F32), mine_end_ref[f].astype(F32)], 0)
            other = other_ref[f].astype(F32)
            at = 2 * f * half
            up_ref[at:at + half] = jnp.where(first, mine, other).astype(BF)
            up_ref[at + half:at + 2 * half] = jnp.where(first, other, mine).astype(BF)
            small = small_ref[f].astype(F32)
            gain_ref[:, f * share:(f + 1) * share] = small[0:1, :share]
            shift_ref[:, f * share:(f + 1) * share] = small[1:2, :share]
        acc_up[...] = jnp.zeros_like(acc_up)
        acc_down[...] = jnp.zeros_like(acc_down)
        dbias_ref[...] = jnp.zeros_like(dbias_ref)
        dgain_ref[...] = jnp.zeros_like(dgain_ref)
        dshift_ref[...] = jnp.zeros_like(dshift_ref)

    xhat, _ = normalize(x_ref[0].astype(F32))
    second = (xhat * gain_ref[...] + shift_ref[...]).astype(BF)
    up = mm(second, up_ref[...], (1, 0)) + upb_ref[...]
    phi = 0.5 * (1.0 + lax.erf(up * (1.0 / math.sqrt(2.0))))
    active = (up * phi).astype(BF)
    slope = phi + up * jnp.exp(-0.5 * up * up) * (1.0 / math.sqrt(2.0 * math.pi))
    tokens = x_ref.shape[1]
    part = mm(active, down_ref[...], (1, 0)).astype(BF)
    grad = g_ref[0]
    back_up = mm(grad, down_ref[...], (1, 1)) * slope
    low_up = back_up.astype(BF)
    dbias_ref[...] += jnp.sum(low_up.astype(F32), 0, keepdims=True)
    acc_up[...] += mm(second, low_up, (0, 0))
    acc_down[...] += mm(active, grad, (0, 0))
    back = mm(low_up, up_ref[...], (1, 1))
    dgain_ref[...] += jnp.sum(back * xhat, 0, keepdims=True)
    dshift_ref[...] += jnp.sum(back, 0, keepdims=True)
    back = (back * gain_ref[...]).astype(BF)
    for k in range(shards):
        @pl.when(step == k)
        def _(k=k):
            outs[k][:tokens] = part
            outs[k][tokens:] = back

    @pl.when(step == pl.num_programs(0) - 1)
    def _():
        if packed:
            owners = dup_ref.shape[0]
            rows = acc_up.shape[0] // shards
            few = rows // owners
            down_rows = acc_down.shape[0] // owners
            for c in range(owners):
                up_rows = [acc_up[f * rows + c * few:f * rows + (c + 1) * few] for f in range(shards)]
                dup_ref[c] = jnp.concatenate(
                    up_rows + [acc_down[c * down_rows:(c + 1) * down_rows]], 0).astype(BF)
            ddown_ref[...] = jnp.zeros_like(ddown_ref)
        else:
            dup_ref[...] = acc_up[...].astype(BF)
            ddown_ref[...] = acc_down[...].astype(BF)


def whole(shape):
    return pl.BlockSpec(shape, lambda *_: (0,) * len(shape))


def cost(macs, size):
    return pl.CostEstimate(flops=int(2 * macs), bytes_accessed=int(size), transcendentals=0)


def feed_forward(at, got, tokens, up_mine, up_other, skip, down, up_bias, owners):
    groups, _, width = got.shape
    hidden = down.shape[0]
    half = width // groups // 2
    quarter = half // 2
    at_up = skip // quarter if up_mine is got else 0
    x_tile = pl.BlockSpec((1, tokens, width), lambda i, at: (at[1] ^ i, 0, 0))
    g_tile = pl.BlockSpec((1, tokens, width), lambda i, at: (at[1] ^ i, 1, 0))
    small_tile = pl.BlockSpec((groups, 16, width), lambda i, at: (0, 2 * tokens // 16, 0))
    row = jax.ShapeDtypeStruct((1, width), F32)
    if owners:
        shapes = [(owners, (width + hidden) // owners, hidden), (16, 128)]
    else:
        shapes = [(width, hidden), (hidden, width)]
    return pl.pallas_call(
        functools.partial(ff_kernel, bool(owners)),
        grid_spec=pltpu.PrefetchScalarGridSpec(
            num_scalar_prefetch=1,
            grid=(groups,),
            in_specs=[x_tile, g_tile, small_tile,
                      pl.BlockSpec((groups, quarter, hidden), lambda i, at: (0, at_up, 0)),
                      pl.BlockSpec((groups, quarter, hidden), lambda i, at: (0, at_up + 1, 0)),
                      whole((groups, half, hidden)), whole((hidden, width)), whole((1, hidden))],
            out_specs=[whole((2 * tokens, width))] * groups + [whole(shape) for shape in shapes]
            + [whole((1, hidden)), whole((1, width)), whole((1, width))],
            scratch_shapes=[pltpu.VMEM((width, hidden), F32), pltpu.VMEM((hidden, width), F32),
                            pltpu.VMEM((width, hidden), BF), pltpu.VMEM((1, width), F32),
                            pltpu.VMEM((1, width), F32)],
        ),
        out_shape=[jax.ShapeDtypeStruct((2 * tokens, width), BF)] * groups
        + [jax.ShapeDtypeStruct(shape, BF) for shape in shapes]
        + [jax.ShapeDtypeStruct((1, hidden), F32), row, row],
        compiler_params=pltpu.CompilerParams(vmem_limit_bytes=VMEM_LIMIT),
        cost_estimate=cost(12 * groups * tokens * width * hidden, 4 * got.size),
        name="feed_forward",
    )(at, got, got, got, up_mine, up_mine, up_other, down, up_bias)


def qkv_kernel(order_ref, xa_ref, xb_ref, ga_ref, gb_ref, w_ref, wo_ref, bias_ref, gain_ref, shift_ref, cos_ref,
               sin_ref, out_ref):
    values = jnp.concatenate([xa_ref[0], xb_ref[0]], 0).astype(F32)
    xhat, _ = normalize(values)
    first = (xhat * gain_ref[...] + shift_ref[...]).astype(BF)
    proj = mm(w_ref[...], first, (1, 1)) + bias_ref[...]
    heads = out_ref.shape[0] // 4
    cosine, sine = cos_ref[0], sin_ref[0]
    for i in range(3 * heads):
        part = proj[i * HEAD:(i + 1) * HEAD]
        if i < 2 * heads:
            part = turn(part, cosine, sine)
        part = part.astype(BF)
        if i < heads:
            part = part * jnp.asarray(1.0 / math.sqrt(HEAD), BF)
        out_ref[i, 0] = part
    back = mm(wo_ref[...], jnp.concatenate([ga_ref[0], gb_ref[0]], 0), (1, 1)).astype(BF)
    for i in range(heads):
        out_ref[3 * heads + i, 0] = back[i * HEAD:(i + 1) * HEAD]


def run_specs(width, held, skip):
    def at(i, order, k):
        run = order[2 * i + k]
        return run // held, run % held + skip, 0

    return [pl.BlockSpec((1, RUN, width), lambda i, order, k=k: at(i, order, k)) for k in (0, 1)]


def project(order, both_all, w, w_out, bias, gain, shift, cosine, sine):
    owners, _, width = both_all.shape
    held = order.shape[0] // owners
    rows, cols = w.shape[0], w_out.shape[0]
    tiles = order.shape[0] // 2
    parts = (rows + cols) // HEAD
    table = pl.BlockSpec((1, HALF, TILE), lambda i, order: (i, 0, 0))
    return pl.pallas_call(
        qkv_kernel,
        grid_spec=pltpu.PrefetchScalarGridSpec(
            num_scalar_prefetch=1,
            grid=(tiles,),
            in_specs=run_specs(width, held, 0) + run_specs(width, held, held)
            + [whole((rows, width)), whole((cols, width)), whole((rows, 1)), whole((1, width)),
               whole((1, width)), table, table],
            out_specs=pl.BlockSpec((parts, 1, HEAD, TILE), lambda i, order: (0, i, 0, 0)),
        ),
        out_shape=jax.ShapeDtypeStruct((parts, tiles, HEAD, TILE), BF),
        compiler_params=pltpu.CompilerParams(vmem_limit_bytes=VMEM_LIMIT),
        cost_estimate=cost(5 * tiles * TILE * width * (rows + cols), 4 * both_all.size),
        name="project",
    )(order, both_all, both_all, both_all, both_all, w, w_out, bias, gain, shift, cosine, sine)


def attention_kernel(share, fused, held, place_ref, q_ref, k_ref, v_ref, d_ref, cos_ref, sin_ref,
                     mix_ref, back_ref, keys, values, dkeys, dvalues, sbuf, pbuf):
    turn_at, step = pl.program_id(0), pl.program_id(1)
    heads, steps = pl.num_programs(0) * fused, pl.num_programs(1)
    tiles = k_ref.shape[1]
    block = share(step, place_ref)
    every = range(fused)

    @pl.when((turn_at == 0) & (step == 0))
    def _():
        mix_ref[...] = jnp.zeros_like(mix_ref)
        back_ref[...] = jnp.zeros_like(back_ref)

    @pl.when(step == 0)
    def _():
        @pl.loop(0, tiles)
        def _(j):
            for h in every:
                keys[h, j] = flip(k_ref[h, j])
                values[h, j] = flip(v_ref[h, j])
                dkeys[h, j] = jnp.zeros((TILE, HEAD), F32)
                dvalues[h, j] = jnp.zeros((TILE, HEAD), F32)

    queries = [q_ref[h, 0] for h in every]

    def fold(x, op):
        return op(x.reshape(TILE // 8, 8, TILE), 0)

    def score(j, peaks):
        new = []
        for h in every:
            s = mm(keys[h, j], queries[h], (1, 0))
            sbuf[h, j] = s
            new.append(jnp.maximum(peaks[h], fold(s, jnp.max)))
        return tuple(new)

    peaks = lax.fori_loop(0, block, score, tuple(jnp.full((8, TILE), NEG, F32) for _ in every))
    key_at = lax.broadcasted_iota(jnp.int32, (TILE, TILE), 0)
    query_at = lax.broadcasted_iota(jnp.int32, (TILE, TILE), 1)
    last = []
    for h in every:
        s = jnp.where(key_at <= query_at, mm(keys[h, block], queries[h], (1, 0)), NEG)
        sbuf[h, block] = s
        last.append(jnp.max(jnp.maximum(peaks[h], fold(s, jnp.max)), 0, keepdims=True))
    peaks = last

    def weigh(j, carry):
        new = []
        for h in every:
            total, mixed = carry[h]
            p = jnp.exp(sbuf[h, j] - peaks[h])
            low = p.astype(BF)
            pbuf[h, j] = low
            new.append((total + fold(p, jnp.sum), mixed + mm(v_ref[h, j], low, (1, 0))))
        return tuple(new)

    sums = lax.fori_loop(
        0, block + 1, weigh,
        tuple((jnp.zeros((8, TILE), F32), jnp.zeros((HEAD, TILE), F32)) for _ in every))
    spreads, backs, back_rows, query_rows = [], [], [], []
    for h in every:
        total, mixed = sums[h]
        inverse = 1.0 / jnp.sum(total, 0, keepdims=True)
        mixed = mixed * inverse
        low_mixed = mixed.astype(BF)
        for k in (0, 1):
            at = place_ref[1 + 2 * block + k]
            mix_ref[at // held, turn_at * fused + h, at % held] = low_mixed[:, k * RUN:(k + 1) * RUN]
        back = d_ref[h, 0].astype(F32) * inverse
        spreads.append(jnp.sum(back * mixed, 0, keepdims=True))
        back = back.astype(BF)
        backs.append(back)
        back_rows.append(flip(back))
        query_rows.append(flip(queries[h]))

    def pull(j, dquery):
        new = []
        for h in every:
            low = pbuf[h, j]
            dp = mm(values[h, j], backs[h], (1, 0))
            ds = (low.astype(F32) * (dp - spreads[h])).astype(BF)
            dvalues[h, j] += mm(low, back_rows[h], (1, 0))
            dkeys[h, j] += mm(ds, query_rows[h], (1, 0))
            new.append(dquery[h] + mm(k_ref[h, j], ds, (1, 0)))
        return tuple(new)

    dquery = lax.fori_loop(0, block + 1, pull, tuple(jnp.zeros((HEAD, TILE), F32) for _ in every))
    for h in every:
        dq = dquery[h] * (1.0 / math.sqrt(HEAD))
        back_ref[turn_at * fused + h, block] = turn(dq, cos_ref[block], -sin_ref[block]).astype(BF)

    @pl.when(step == steps - 1)
    def _():
        @pl.loop(0, tiles)
        def _(j):
            for h in every:
                at = heads + turn_at * fused + h
                back_ref[at, j] = turn(dkeys[h, j].T, cos_ref[j], -sin_ref[j]).astype(BF)
                back_ref[heads + at, j] = dvalues[h, j].T.astype(BF)


def attend(place, qkv, cosine, sine, owners, sharers):
    parts, tiles, _, _ = qkv.shape
    heads = parts // 4
    held = (place.shape[0] - 1) // owners
    steps = tiles // sharers
    fused = heads if tiles <= 16 else 1
    turns = heads // fused

    def share(step, place_ref):
        return 2 * sharers * (step // 2) + jnp.where(step % 2 == 0, place_ref[0], 2 * sharers - 1 - place_ref[0])

    all_tiles, one_tile = (fused, tiles, HEAD, TILE), (fused, 1, HEAD, TILE)
    return pl.pallas_call(
        functools.partial(attention_kernel, share, fused, held),
        grid_spec=pltpu.PrefetchScalarGridSpec(
            num_scalar_prefetch=1,
            grid=(turns, steps),
            in_specs=[
                pl.BlockSpec(one_tile, lambda h, n, p: (h, share(n, p), 0, 0)),
                pl.BlockSpec(all_tiles, lambda h, n, p: (turns + h, 0, 0, 0)),
                pl.BlockSpec(all_tiles, lambda h, n, p: (2 * turns + h, 0, 0, 0)),
                pl.BlockSpec(one_tile, lambda h, n, p: (3 * turns + h, share(n, p), 0, 0)),
                whole((tiles, HALF, TILE)),
                whole((tiles, HALF, TILE)),
            ],
            out_specs=[whole((owners, heads, held, HEAD, RUN)), whole((3 * heads, tiles, HEAD, TILE))],
            scratch_shapes=[
                pltpu.VMEM((fused, tiles, TILE, HEAD), BF),
                pltpu.VMEM((fused, tiles, TILE, HEAD), BF),
                pltpu.VMEM((fused, tiles, TILE, HEAD), F32),
                pltpu.VMEM((fused, tiles, TILE, HEAD), F32),
                pltpu.VMEM((fused, tiles, TILE, TILE), F32),
                pltpu.VMEM((fused, tiles, TILE, TILE), BF),
            ],
        ),
        out_shape=[jax.ShapeDtypeStruct((owners, heads, held, HEAD, RUN), BF),
                   jax.ShapeDtypeStruct((3 * heads, tiles, HEAD, TILE), BF)],
        compiler_params=pltpu.CompilerParams(vmem_limit_bytes=VMEM_LIMIT),
        cost_estimate=cost(40 * heads * HEAD * tiles * TILE * steps * TILE, 4 * qkv.size),
        name="attend",
    )(place, qkv, qkv, qkv, qkv, cosine, sine)


def back_weight_kernel(order_ref, b_ref, w_ref, xa_ref, xb_ref, ga_ref, gb_ref, ma_ref, mb_ref, gain_ref, shift_ref,
                       _, __, dw_ref, dout_ref, dbias_ref, dgain_ref, dshift_ref, acc):
    step = pl.program_id(0)

    @pl.when(step == 0)
    def _():
        acc[...] = jnp.zeros_like(acc)
        dout_ref[...] = jnp.zeros_like(dout_ref)
        dbias_ref[...] = jnp.zeros_like(dbias_ref)

    xhat, _ = normalize(jnp.concatenate([xa_ref[0], xb_ref[0]], 0).astype(F32))
    rows, cols = b_ref.shape[0] * HEAD, ma_ref.shape[1] * HEAD
    back = b_ref[...].reshape(rows, TILE)
    acc[...] += mm(back, xhat.astype(BF), (1, 0))
    mixed = jnp.concatenate([r[0, :, 0].reshape(cols, RUN) for r in (ma_ref, mb_ref)], 1)
    dout_ref[...] += mm(mixed, jnp.concatenate([ga_ref[0], gb_ref[0]], 0), (1, 0))
    dbias_ref[...] += jnp.sum(back.astype(F32), 1, keepdims=True)

    @pl.when(step == pl.num_programs(0) - 1)
    def _():
        weight = w_ref[...].astype(F32)
        bias = dbias_ref[...]
        dgain_ref[...] = jnp.sum(acc[...] * weight, 0, keepdims=True)
        dshift_ref[...] = jnp.sum(bias * weight, 0, keepdims=True)
        dw_ref[...] = (acc[...] * gain_ref[...] + bias * shift_ref[...]).T.astype(BF)


def back_input_kernel(order_ref, b_ref, w_ref, gain_ref, _, __, e_ref):
    step = pl.program_id(0)
    back = b_ref[...].reshape(b_ref.shape[0] * HEAD, TILE)
    e = (mm(back, w_ref[...], (0, 0)) * gain_ref[...]).astype(BF)
    e_ref[order_ref[2 * step]] = e[:RUN]
    e_ref[order_ref[2 * step + 1]] = e[RUN:]


ANY = pl.BlockSpec(memory_space=pl.ANY)


def back_to_weight(order, back, w, both_all, mixed, gain, shift, earlier):
    owners, _, width = both_all.shape
    held = order.shape[0] // owners
    rows = w.shape[0]
    parts, tiles, _, _ = back.shape
    heads = parts // 3
    line = jax.ShapeDtypeStruct((1, width), F32)

    def mixed_at(i, order, k):
        run = order[2 * i + k]
        return run // held, 0, run % held, 0, 0

    mixed_specs = [pl.BlockSpec((1, heads, 1, HEAD, RUN), lambda i, order, k=k: mixed_at(i, order, k)) for k in (0, 1)]
    return pl.pallas_call(
        back_weight_kernel,
        grid_spec=pltpu.PrefetchScalarGridSpec(
            num_scalar_prefetch=1,
            grid=(tiles,),
            in_specs=[pl.BlockSpec((parts, 1, HEAD, TILE), lambda i, order: (0, i, 0, 0)), whole((rows, width))]
            + run_specs(width, held, 0) + run_specs(width, held, held) + mixed_specs
            + [whole((1, width)), whole((1, width)), ANY, ANY],
            out_specs=[whole((width, rows)), whole((heads * HEAD, width)), whole((rows, 1)), whole((1, width)),
                       whole((1, width))],
            scratch_shapes=[pltpu.VMEM((rows, width), F32)],
        ),
        out_shape=[jax.ShapeDtypeStruct((width, rows), BF), jax.ShapeDtypeStruct((heads * HEAD, width), F32),
                   jax.ShapeDtypeStruct((rows, 1), F32), line, line],
        compiler_params=pltpu.CompilerParams(vmem_limit_bytes=VMEM_LIMIT),
        cost_estimate=cost(5 * tiles * TILE * width * rows, 4 * both_all.size),
        name="back_to_weight",
    )(order, back, w, both_all, both_all, both_all, both_all, mixed, mixed, gain, shift, *earlier)


def back_to_input(order, back, w, gain, earlier):
    rows, width = w.shape
    parts, tiles, _, _ = back.shape
    runs = order.shape[0]
    return pl.pallas_call(
        back_input_kernel,
        grid_spec=pltpu.PrefetchScalarGridSpec(
            num_scalar_prefetch=1,
            grid=(tiles,),
            in_specs=[pl.BlockSpec((parts, 1, HEAD, TILE), lambda i, order: (0, i, 0, 0)), whole((rows, width)),
                      whole((1, width)), ANY, ANY],
            out_specs=whole((runs, RUN, width)),
        ),
        out_shape=jax.ShapeDtypeStruct((runs, RUN, width), BF),
        compiler_params=pltpu.CompilerParams(vmem_limit_bytes=VMEM_LIMIT),
        cost_estimate=cost(5 * tiles * TILE * width * rows, 8 * back.size),
        name="back_to_input",
    )(order, back, w, gain, *earlier)


def ff_place_kernel(at_ref, all_ref, up_ref, down_ref):
    step_rows, shards = up_ref.shape[0], up_ref.shape[1] // all_ref.shape[2]
    hidden = all_ref.shape[2]
    value = all_ref[0].astype(F32)
    for k in range(shards):
        at = pl.multiple_of((at_ref[0] ^ k) * hidden, hidden)
        up_ref[:, pl.ds(at, hidden)] = value[k * step_rows:(k + 1) * step_rows]
    down_ref[...] = value[shards * step_rows:]


def place_ff(at, gathered, shards, step_rows):
    owners, rows, width = gathered.shape
    down_rows = rows - shards * step_rows
    return pl.pallas_call(
        ff_place_kernel,
        grid_spec=pltpu.PrefetchScalarGridSpec(
            num_scalar_prefetch=1,
            grid=(owners,),
            in_specs=[pl.BlockSpec((1, rows, width), lambda i, at: (i, 0, 0))],
        out_specs=[pl.BlockSpec((step_rows, shards * width), lambda i, core: (i, 0)),
                       pl.BlockSpec((down_rows, width), lambda i, core: (i, 0))],
        ),
        out_shape=[jax.ShapeDtypeStruct((owners * step_rows, shards * width), F32),
                   jax.ShapeDtypeStruct((owners * down_rows, width), F32)],
        compiler_params=pltpu.CompilerParams(vmem_limit_bytes=VMEM_LIMIT),
        name="place_ff",
    )(at, gathered)


def io_place_kernel(cols, core_ref, mine_ref, other_ref, in_ref, out_ref, line_ref):
    parity = pl.program_id(0)
    own = parity == core_ref[0]
    count, rows, width = mine_ref.shape
    half = rows // 2
    groups = width // cols
    held = count // groups
    for g in range(groups):
        value = None
        for i in range(held):
            at = g * held + i
            one = jnp.where(own, mine_ref[at].astype(F32), other_ref[at].astype(F32))
            value = one if value is None else value + one
        for part in range(3):
            at = part * width + g * cols
            in_ref[:, at:at + cols] = value[half:, part * cols:(part + 1) * cols]
        if g == 0:
            out_ref[...] = value[:half]
            line_ref[...] = value[half:, 3 * cols:]
        else:
            out_ref[...] += value[:half]
            line_ref[...] += value[half:, 3 * cols:]


def place_io(core, mine, other, cols):
    count, rows, width = mine.shape
    half = rows // 2
    return pl.pallas_call(
        functools.partial(io_place_kernel, cols),
        grid_spec=pltpu.PrefetchScalarGridSpec(
            num_scalar_prefetch=1,
            grid=(2,),
            in_specs=[whole(mine.shape), whole(other.shape)],
            out_specs=[pl.BlockSpec((half, 3 * width), lambda i, core: (i, 0)),
                       pl.BlockSpec((half, width), lambda i, core: (i, 0)),
                       pl.BlockSpec((half, width - 3 * cols), lambda i, core: (i, 0))],
        ),
        out_shape=[jax.ShapeDtypeStruct((rows, 3 * width), F32), jax.ShapeDtypeStruct((rows, width), F32),
                   jax.ShapeDtypeStruct((rows, width - 3 * cols), F32)],
        compiler_params=pltpu.CompilerParams(vmem_limit_bytes=VMEM_LIMIT),
        name="place_io",
    )(core[None], mine, other)


def spread_out(pieces, axis, groups=None):
    return lax.all_to_all(pieces, axis, 0, 0, axis_index_groups=groups)


def to_all_value(x, count):
    return jnp.broadcast_to(x[None], (count,) + x.shape)


def to_all(x, axis, groups=None, count=None):
    return spread_out(to_all_value(x, count or lax.axis_size(axis)), axis, groups)


def at_distance(pieces):
    count = len(pieces)
    return [pieces[0]] + [
        lax.ppermute(pieces[k], "fsdp", [(i, i ^ k) for i in range(count)]) for k in range(1, count)]


def by_distance(pieces, shard):
    return at_distance([
        lax.dynamic_index_in_dim(pieces, shard ^ k, 0, keepdims=False) for k in range(pieces.shape[0])])


def total(values):
    result = values[0].astype(F32)
    for v in values[1:]:
        result = result + v.astype(F32)
    return result


def after(index, value):
    first = value[(0,) * value.ndim]
    return index + (first != first).astype(jnp.int32)


def on_device(
    inputs, positions, in_weight, in_bias, out_weight, out_bias, up_weight, up_bias, down_weight, down_bias,
    first_gain, first_shift, second_gain, second_shift, out_grad,
):
    x, grad, place = inputs[0], out_grad[0], positions[0]
    tokens, width = x.shape
    owners, shards = lax.axis_size("ctx"), lax.axis_size("fsdp")
    here, shard = lax.axis_index("ctx"), lax.axis_index("fsdp")
    heads = width // HEAD
    groups = math.gcd(heads, owners // 2)
    sharers = owners // groups
    own_heads = heads // groups
    cols = own_heads * HEAD
    group, sharer, core = here // sharers, here % sharers, here % 2
    hidden = down_weight.shape[0]
    rows = in_weight.shape[0]
    half = rows // 2
    length = tokens * owners
    held = tokens // RUN
    joined = hidden == width
    tiles = length // TILE
    parity = [[i for i in range(owners) if i % 2 == k] for k in (0, 1)]
    pairs = [(i, i ^ 1) for i in range(owners)]

    def swap(value):
        return lax.ppermute(value, "ctx", pairs)

    def both(mine, other):
        return jnp.stack([jnp.where(core == 0, mine, other), jnp.where(core == 0, other, mine)], 1)

    run_rows = jnp.broadcast_to(jnp.pad((place[::RUN] // RUN).astype(BF), (0, width - held))[None], (16, width))
    both_all = lax.all_gather(jnp.concatenate([x, grad, run_rows], 0), "ctx", axis=0, tiled=False)

    def block(values):
        lines = [jnp.pad(v[None], ((0, 0), (0, width - v.shape[0]))) for v in values]
        return jnp.pad(jnp.concatenate(lines, 0), ((0, 16 - len(values)), (0, 0)))

    small_block = block([second_gain, second_shift])
    smalls = [in_bias, out_bias, down_bias, first_gain, first_shift]

    def own_half(value, at=core):
        return lax.dynamic_slice_in_dim(value, at * half, half, 0)

    up_pieces = own_half(up_weight).reshape(half, shards, hidden).transpose(1, 0, 2)
    shared = to_all_value(jnp.concatenate([x, grad, small_block], 0), shards)
    skip = -(-(2 * tokens + 16) // (half // 2)) * (half // 2)
    if joined:
        gap = jnp.zeros((shards, skip - 2 * tokens - 16, width), BF)
        plane = spread_out(jnp.concatenate([shared, gap, up_pieces], 1), "fsdp")
        up_own = plane[:, skip:]
    else:
        plane, up_own = spread_out(shared, "fsdp"), spread_out(up_pieces, "fsdp")
    later = after(core, plane)
    in_own = own_half(in_weight, later).reshape(half, 3, groups, cols)
    in_own = lax.dynamic_index_in_dim(in_own, group, 2, keepdims=False).reshape(half, 3 * cols)
    in_own = jnp.pad(in_own, ((0, 0), (0, width - 3 * cols)))
    io_send = to_all_value(jnp.concatenate([own_half(out_weight, later), in_own, block(smalls)], 0), shards)
    io_got = spread_out(io_send, "fsdp")
    small_got, io_got = io_got[:, 2 * half:].astype(F32), io_got[:, :2 * half]

    full_in_bias, full_out_bias, full_down_bias, gain_one, shift_one = [
        small_got[:, i, :s.shape[0]].reshape(-1) for i, s in enumerate(smalls)]

    small_step = rows // owners
    packed = joined and small_step % 8 == 0
    up_other, up_bias_row = swap(up_own), up_bias.astype(F32)[None]
    *ff_parts, up_part, down_part, up_bias_part, gain_two_part, shift_two_part = feed_forward(
        jnp.stack([core, shard]), plane, tokens, plane if joined else up_own, up_other, skip, down_weight,
        up_bias_row, owners if packed else 0)

    def give_half(pieces, axis, mine=core):
        keep = lax.dynamic_index_in_dim(pieces, mine, axis, keepdims=False)
        give = lax.dynamic_index_in_dim(pieces, 1 - mine, axis, keepdims=False)
        return (keep.astype(F32) + swap(give).astype(F32)).astype(BF)

    def reduce_owners(pieces):
        return lax.psum_scatter(pieces, "ctx", scatter_dimension=0, tiled=False)

    def gather_owners(value):
        mine = to_all(value, "ctx", parity, owners // 2)
        return mine, swap(mine)

    cut = shards * small_step
    if packed:
        summed = reduce_owners(up_part + after(after(jnp.int32(0), both_all), io_got).astype(BF))
        up_sum, down_sum = summed[:cut], summed[cut:]
    else:
        up_pieces = up_part.reshape(shards, owners, small_step, hidden).transpose(1, 0, 2, 3)
        up_sum = reduce_owners(up_pieces.reshape(owners, cut, hidden))
        down_sum = reduce_owners(down_part.reshape(owners, hidden // owners, width))

    io_full = both(io_got, swap(io_got)).reshape(shards, 2, 2, half, width)
    out_full = io_full[:, :, 0].reshape(width, width)
    in_full = io_full[:, :, 1].reshape(width, width)[:, :3 * cols].T
    out_own = lax.dynamic_slice_in_dim(out_full, group * cols, cols, 0)
    run_at = both_all[:, 2 * tokens, :held].reshape(-1).astype(jnp.int32)
    runs = run_at.shape[0]
    at_run = lax.broadcasted_iota(jnp.int32, (runs, runs), 0)
    of_run = lax.broadcasted_iota(jnp.int32, (runs, runs), 1)
    order = jnp.sum(jnp.where(run_at[None] == at_run, of_run, 0), 1)

    ladder = 10000.0 ** (-jnp.arange(0, ROT, 2, dtype=F32) / ROT)
    angle = jnp.arange(length, dtype=jnp.int32).astype(F32).reshape(tiles, 1, TILE) * ladder[None, :, None]
    cosine, sine = jnp.cos(angle), jnp.sin(angle)

    bias_own = lax.dynamic_index_in_dim(full_in_bias.reshape(3, groups, cols), group, 1, keepdims=False)
    qkv = project(order, both_all, in_full, out_own, bias_own.reshape(-1, 1), gain_one[None], shift_one[None],
                  cosine, sine)
    spots = jnp.concatenate([sharer[None].astype(jnp.int32), order])
    ff_got = at_distance(ff_parts)
    mixed_out, back_qkv = attend(spots, qkv, cosine, sine, owners, sharers)
    up_sum = jnp.concatenate(by_distance(up_sum.reshape(shards, small_step, hidden), after(shard, back_qkv)), 0)
    mixed_own = give_half(mixed_out.reshape(owners // 2, 2, own_heads, held, HEAD, RUN), 1)
    mixed_got = spread_out(mixed_own, "ctx", parity)
    if joined:
        ff_own = jnp.concatenate([up_sum, down_sum], 0)
        ff_all = lax.all_gather(ff_own, "ctx", axis=0, tiled=False)
        up_all, down_all = ff_all[:, :cut], ff_all[:, cut:]
    else:
        ff_own = up_sum
        up_all, down_all = [lax.all_gather(v, "ctx", axis=0, tiled=False) for v in (up_sum, down_sum)]
    gain_row, shift_row = gain_one[None], shift_one[None]
    in_part, out_part, in_bias_part, gain_one_part, shift_one_part = back_to_weight(
        order, back_qkv, in_full, both_all, mixed_out, gain_row, shift_row, (mixed_own, ff_own))
    e_runs = back_to_input(order, back_qkv, in_full, gain_row, (in_part, mixed_got))
    e_sum = lax.psum_scatter(e_runs.reshape(length, width), "ctx", scatter_dimension=0, tiled=True)

    if packed:
        up_weight_gradient, down_weight_gradient = place_ff(shard[None], ff_all, shards, small_step)
    else:
        up_all = up_all.reshape(owners, shards, small_step, hidden)
        up_all = [lax.dynamic_index_in_dim(up_all, shard ^ f, 1, keepdims=False) for f in range(shards)]
        up_weight_gradient = jnp.concatenate(up_all, -1).reshape(rows, shards * hidden).astype(F32)
        down_weight_gradient = down_all.reshape(hidden, width).astype(F32)

    ff_sum = total(ff_got) + after(jnp.int32(0), down_weight_gradient).astype(F32)
    x32, grad32 = x.astype(F32), grad.astype(F32)
    mixed = jnp.sum(mixed_got.astype(F32).reshape(groups, sharers // 2, own_heads, held, HEAD, RUN), 1)
    mixed = mixed.transpose(0, 1, 3, 2, 4).reshape(width, tokens).astype(BF)
    branch = mm(mixed, out_full, (0, 0))
    output = x32 + (branch + full_out_bias) + (ff_sum[:tokens] + full_down_bias)

    in_bias_full = lax.dynamic_update_slice_in_dim(
        jnp.zeros((3, groups, cols), F32), in_bias_part.reshape(3, 1, cols), group, 1)
    lines = [in_bias_full.reshape(-1), jnp.sum(grad32, 0), gain_one_part[0], shift_one_part[0], gain_two_part[0],
             shift_two_part[0]]
    lines = [v.reshape(shards, -1) for v in lines]
    at_shard = (jnp.arange(shards) == shard)[:, None]
    lines.append(jnp.where(at_shard, up_bias_part, 0.0))
    line_sizes = [v.shape[1] for v in lines]
    lines = jnp.concatenate(lines, 1).astype(BF).reshape(shards, 2, -1, width - 3 * cols)
    line_rows = lines.shape[2]
    lines = jnp.pad(lines, ((0, 0), (0, 0), (0, half - line_rows), (0, 0)))
    out_rows = lax.dynamic_update_slice_in_dim(
        jnp.zeros((width, width), BF), out_part.astype(BF), group * cols, 0)
    in_pieces = jnp.concatenate([in_part.reshape(shards, 2, half, 3 * cols), lines], 3)
    pieces = jnp.concatenate([out_rows.reshape(shards, 2, half, width), in_pieces], 2)
    pieces = give_half(pieces, 1)
    pieces = total(by_distance(pieces, shard)).astype(BF)
    pieces = pieces + after(jnp.int32(0), down_weight_gradient).astype(BF)
    in_weight_gradient, out_weight_gradient, line_sum = place_io(
        core, *gather_owners(pieces), cols)
    line_sum = line_sum.reshape(2, half, -1)[:, :line_rows].reshape(-1)
    totals, at = [], 0
    for size in line_sizes:
        totals.append(line_sum[at:at + size])
        at += size

    e = e_sum.astype(F32) + ff_sum[tokens:]
    xhat, inverse = normalize(x32)
    input_gradient = grad32 + inverse * (
        e - jnp.mean(e, -1, keepdims=True) - xhat * jnp.mean(e * xhat, -1, keepdims=True))
    return (
        output.astype(BF)[None], input_gradient[None], in_weight_gradient, totals[0], out_weight_gradient, totals[1],
        up_weight_gradient, totals[6], down_weight_gradient, totals[1], totals[2], totals[3], totals[4], totals[5],
    )


def solution(mesh):
    token, matrix, vector = P("fsdp", "ctx", None), P("fsdp", None), P("fsdp")
    return jax.shard_map(
        on_device,
        mesh=mesh,
        in_specs=(token, P("fsdp", "ctx"), matrix, vector, matrix, vector, matrix, vector, matrix, vector,
                  vector, vector, vector, vector, token),
        out_specs=(token, token, matrix, vector, matrix, vector, matrix, vector, matrix, vector,
                   vector, vector, vector, vector),
        check_vma=False,
    )
```

```python
import functools
import math

import jax
import jax.numpy as jnp
from jax import lax
from jax.experimental import pallas as pl
from jax.experimental.pallas import tpu as pltpu
from jax.sharding import PartitionSpec as P

HEAD = 64
ROT = 16
HALF = ROT // 2
RUN = 128
TILE = 256
SUB = 256
NEG = -1e30
EPS = 1e-05
BF = jnp.bfloat16
F32 = jnp.float32
VMEM_LIMIT = 60 * 1024 * 1024


def mm(left, right, dims):
    return lax.dot_general(left, right, ((dims[:1], dims[1:]), ((), ())), preferred_element_type=F32)


def flip(x):
    return x.astype(F32).T.astype(x.dtype)


def normalize(values):
    mean = jnp.mean(values, -1, keepdims=True)
    centred = values - mean
    spread = jnp.mean(centred * centred, -1, keepdims=True)
    inverse = lax.rsqrt(spread + EPS)
    return centred * inverse, inverse


def turn(values, cosine, sine):
    one, two = values[:HALF], values[HALF:ROT]
    return jnp.concatenate([one * cosine - two * sine, two * cosine + one * sine, values[ROT:]], 0)


def ff_kernel(packed, core_ref, x_ref, g_ref, small_ref, mine_ref, mine_end_ref, other_ref, down_ref, upb_ref,
              *refs):
    shards = small_ref.shape[0]
    outs, refs = refs[:shards], refs[shards:]
    (dup_ref, ddown_ref, dbias_ref, dgain_ref, dshift_ref, acc_up, acc_down, up_ref, gain_ref, shift_ref) = refs
    step = pl.program_id(0)

    @pl.when(step == 0)
    def _():
        half = other_ref.shape[1]
        share = gain_ref.shape[1] // shards
        first = core_ref[0] == 0
        for f in range(shards):
            mine = jnp.concatenate([mine_ref[f].astype(F32), mine_end_ref[f].astype(F32)], 0)
            other = other_ref[f].astype(F32)
            at = 2 * f * half
            up_ref[at:at + half] = jnp.where(first, mine, other).astype(BF)
            up_ref[at + half:at + 2 * half] = jnp.where(first, other, mine).astype(BF)
            small = small_ref[f].astype(F32)
            gain_ref[:, f * share:(f + 1) * share] = small[0:1, :share]
            shift_ref[:, f * share:(f + 1) * share] = small[1:2, :share]
        acc_up[...] = jnp.zeros_like(acc_up)
        acc_down[...] = jnp.zeros_like(acc_down)
        dbias_ref[...] = jnp.zeros_like(dbias_ref)
        dgain_ref[...] = jnp.zeros_like(dgain_ref)
        dshift_ref[...] = jnp.zeros_like(dshift_ref)

    xhat, _ = normalize(x_ref[0].astype(F32))
    second = (xhat * gain_ref[...] + shift_ref[...]).astype(BF)
    up = mm(second, up_ref[...], (1, 0)) + upb_ref[...]
    phi = 0.5 * (1.0 + lax.erf(up * (1.0 / math.sqrt(2.0))))
    active = (up * phi).astype(BF)
    slope = phi + up * jnp.exp(-0.5 * up * up) * (1.0 / math.sqrt(2.0 * math.pi))
    tokens = x_ref.shape[1]
    part = mm(active, down_ref[...], (1, 0)).astype(BF)
    grad = g_ref[0]
    back_up = mm(grad, down_ref[...], (1, 1)) * slope
    low_up = back_up.astype(BF)
    dbias_ref[...] += jnp.sum(low_up.astype(F32), 0, keepdims=True)
    acc_up[...] += mm(second, low_up, (0, 0))
    acc_down[...] += mm(active, grad, (0, 0))
    back = mm(low_up, up_ref[...], (1, 1))
    dgain_ref[...] += jnp.sum(back * xhat, 0, keepdims=True)
    dshift_ref[...] += jnp.sum(back, 0, keepdims=True)
    back = (back * gain_ref[...]).astype(BF)
    for k in range(shards):
        @pl.when(step == k)
        def _(k=k):
            outs[k][:tokens] = part
            outs[k][tokens:] = back

    @pl.when(step == pl.num_programs(0) - 1)
    def _():
        if packed:
            owners = dup_ref.shape[0]
            rows = acc_up.shape[0] // shards
            few = rows // owners
            down_rows = acc_down.shape[0] // owners
            for c in range(owners):
                up_rows = [acc_up[f * rows + c * few:f * rows + (c + 1) * few] for f in range(shards)]
                dup_ref[c] = jnp.concatenate(
                    up_rows + [acc_down[c * down_rows:(c + 1) * down_rows]], 0).astype(BF)
            ddown_ref[...] = jnp.zeros_like(ddown_ref)
        else:
            dup_ref[...] = acc_up[...].astype(BF)
            ddown_ref[...] = acc_down[...].astype(BF)


ANY = pl.BlockSpec(memory_space=pl.ANY)


def whole(shape):
    return pl.BlockSpec(shape, lambda *_: (0,) * len(shape))


def cost(macs, size):
    return pl.CostEstimate(flops=int(2 * macs), bytes_accessed=int(size), transcendentals=0)


def feed_forward(at, got, tokens, up_mine, up_other, skip, down, up_bias, owners):
    groups, _, width = got.shape
    hidden = down.shape[0]
    half = width // groups // 2
    quarter = half // 2
    at_up = skip // quarter if up_mine is got else 0
    x_tile = pl.BlockSpec((1, tokens, width), lambda i, at: (at[1] ^ i, 0, 0))
    g_tile = pl.BlockSpec((1, tokens, width), lambda i, at: (at[1] ^ i, 1, 0))
    small_tile = pl.BlockSpec((groups, 16, width), lambda i, at: (0, 2 * tokens // 16, 0))
    row = jax.ShapeDtypeStruct((1, width), F32)
    if owners:
        shapes = [(owners, (width + hidden) // owners, hidden), (16, 128)]
    else:
        shapes = [(width, hidden), (hidden, width)]
    return pl.pallas_call(
        functools.partial(ff_kernel, bool(owners)),
        grid_spec=pltpu.PrefetchScalarGridSpec(
            num_scalar_prefetch=1,
            grid=(groups,),
            in_specs=[x_tile, g_tile, small_tile,
                      pl.BlockSpec((groups, quarter, hidden), lambda i, at: (0, at_up, 0)),
                      pl.BlockSpec((groups, quarter, hidden), lambda i, at: (0, at_up + 1, 0)),
                      whole((groups, half, hidden)), whole((hidden, width)), whole((1, hidden))],
            out_specs=[whole((2 * tokens, width))] * groups + [whole(shape) for shape in shapes]
            + [whole((1, hidden)), whole((1, width)), whole((1, width))],
            scratch_shapes=[pltpu.VMEM((width, hidden), F32), pltpu.VMEM((hidden, width), F32),
                            pltpu.VMEM((width, hidden), BF), pltpu.VMEM((1, width), F32),
                            pltpu.VMEM((1, width), F32)],
        ),
        out_shape=[jax.ShapeDtypeStruct((2 * tokens, width), BF)] * groups
        + [jax.ShapeDtypeStruct(shape, BF) for shape in shapes]
        + [jax.ShapeDtypeStruct((1, hidden), F32), row, row],
        compiler_params=pltpu.CompilerParams(vmem_limit_bytes=VMEM_LIMIT),
        cost_estimate=cost(12 * groups * tokens * width * hidden, 4 * got.size),
        name="feed_forward",
    )(at, got, got, got, up_mine, up_mine, up_other, down, up_bias)


def qkv_kernel(order_ref, xa_ref, xb_ref, ga_ref, gb_ref, w_ref, wo_ref, bias_ref, gain_ref, shift_ref, cos_ref,
               sin_ref, out_ref):
    values = jnp.concatenate([xa_ref[0], xb_ref[0]], 0).astype(F32)
    xhat, _ = normalize(values)
    first = (xhat * gain_ref[...] + shift_ref[...]).astype(BF)
    proj = mm(w_ref[...], first, (1, 1)) + bias_ref[...]
    heads = out_ref.shape[0] // 4
    cosine, sine = cos_ref[0], sin_ref[0]
    for i in range(3 * heads):
        part = proj[i * HEAD:(i + 1) * HEAD]
        if i < 2 * heads:
            part = turn(part, cosine, sine)
        part = part.astype(BF)
        if i < heads:
            part = part * jnp.asarray(1.0 / math.sqrt(HEAD), BF)
        out_ref[i, 0] = part
    back = mm(wo_ref[...], jnp.concatenate([ga_ref[0], gb_ref[0]], 0), (1, 1)).astype(BF)
    for i in range(heads):
        out_ref[3 * heads + i, 0] = back[i * HEAD:(i + 1) * HEAD]


def run_specs(width, held, skip):
    def at(i, order, k):
        run = order[2 * i + k]
        return run // held, run % held + skip, 0

    return [pl.BlockSpec((1, RUN, width), lambda i, order, k=k: at(i, order, k)) for k in (0, 1)]


def project(order, both_all, w, w_out, bias, gain, shift, cosine, sine):
    owners, _, width = both_all.shape
    held = order.shape[0] // owners
    rows, cols = w.shape[0], w_out.shape[0]
    tiles = order.shape[0] // 2
    parts = (rows + cols) // HEAD
    table = pl.BlockSpec((1, HALF, TILE), lambda i, order: (i, 0, 0))
    return pl.pallas_call(
        qkv_kernel,
        grid_spec=pltpu.PrefetchScalarGridSpec(
            num_scalar_prefetch=1,
            grid=(tiles,),
            in_specs=run_specs(width, held, 0) + run_specs(width, held, held)
            + [whole((rows, width)), whole((cols, width)), whole((rows, 1)), whole((1, width)),
               whole((1, width)), table, table],
            out_specs=pl.BlockSpec((parts, 1, HEAD, TILE), lambda i, order: (0, i, 0, 0)),
        ),
        out_shape=jax.ShapeDtypeStruct((parts, tiles, HEAD, TILE), BF),
        compiler_params=pltpu.CompilerParams(vmem_limit_bytes=VMEM_LIMIT),
        cost_estimate=cost(5 * tiles * TILE * width * (rows + cols), 4 * both_all.size),
        name="project",
    )(order, both_all, both_all, both_all, both_all, w, w_out, bias, gain, shift, cosine, sine)


def attention_kernel(share, fused, held, place_ref, q_ref, k_ref, v_ref, d_ref, cos_ref, sin_ref,
                     mix_ref, back_ref, keys, values, dkeys, dvalues, sbuf, pbuf):
    turn_at, step = pl.program_id(0), pl.program_id(1)
    heads, steps = pl.num_programs(0) * fused, pl.num_programs(1)
    tiles = k_ref.shape[1]
    block = share(step, place_ref)
    every = range(fused)

    @pl.when((turn_at == 0) & (step == 0))
    def _():
        mix_ref[...] = jnp.zeros_like(mix_ref)
        back_ref[...] = jnp.zeros_like(back_ref)

    @pl.when(step == 0)
    def _():
        @pl.loop(0, tiles)
        def _(j):
            for h in every:
                keys[h, j] = flip(k_ref[h, j])
                values[h, j] = flip(v_ref[h, j])
                dkeys[h, j] = jnp.zeros((TILE, HEAD), F32)
                dvalues[h, j] = jnp.zeros((TILE, HEAD), F32)

    queries = [q_ref[h, 0] for h in every]

    def fold(x, op):
        return op(x.reshape(x.shape[0] // 8, 8, TILE), 0)

    pieces = [(h, slice(i, i + SUB)) for h in every for i in range(0, TILE, SUB)]

    def score(j, peaks):
        new = list(peaks)
        for h, at in pieces:
            s = mm(keys[h, j, at], queries[h], (1, 0))
            sbuf[h, j, at] = s
            new[h] = jnp.maximum(new[h], fold(s, jnp.max))
        return tuple(new)

    peaks = lax.fori_loop(0, block, score, tuple(jnp.full((8, TILE), NEG, F32) for _ in every))
    key_at = lax.broadcasted_iota(jnp.int32, (TILE, TILE), 0)
    query_at = lax.broadcasted_iota(jnp.int32, (TILE, TILE), 1)
    last = []
    for h in every:
        s = jnp.where(key_at <= query_at, mm(keys[h, block], queries[h], (1, 0)), NEG)
        sbuf[h, block] = s
        last.append(jnp.max(jnp.maximum(peaks[h], fold(s, jnp.max)), 0, keepdims=True))
    peaks = last

    def weigh(j, carry):
        new = list(carry)
        for h, at in pieces:
            total, mixed = new[h]
            p = jnp.exp(sbuf[h, j, at] - peaks[h])
            low = p.astype(BF)
            pbuf[h, j, at] = low
            new[h] = (total + fold(p, jnp.sum), mixed)
        for h, at in pieces:
            total, mixed = new[h]
            new[h] = (total, mixed + mm(v_ref[h, j, :, at], pbuf[h, j, at], (1, 0)))
        return tuple(new)

    sums = lax.fori_loop(
        0, block + 1, weigh,
        tuple((jnp.zeros((8, TILE), F32), jnp.zeros((HEAD, TILE), F32)) for _ in every))
    spreads, backs, back_rows, query_rows = [], [], [], []
    for h in every:
        total, mixed = sums[h]
        inverse = 1.0 / jnp.sum(total, 0, keepdims=True)
        mixed = mixed * inverse
        low_mixed = mixed.astype(BF)
        for k in (0, 1):
            at = place_ref[1 + 2 * block + k]
            mix_ref[at // held, turn_at * fused + h, at % held] = low_mixed[:, k * RUN:(k + 1) * RUN]
        back = d_ref[h, 0].astype(F32) * inverse
        spreads.append(jnp.sum(back * mixed, 0, keepdims=True))
        back = back.astype(BF)
        backs.append(back)
        back_rows.append(flip(back))
        query_rows.append(flip(queries[h]))

    def pull(j, dquery):
        new = list(dquery)

        def finish(h, at, dp):
            low = pbuf[h, j, at]
            ds = (low.astype(F32) * (dp - spreads[h])).astype(BF)
            dvalues[h, j, at] += mm(low, back_rows[h], (1, 0))
            dkeys[h, j, at] += mm(ds, query_rows[h], (1, 0))
            new[h] = new[h] + mm(k_ref[h, j, :, at], ds, (1, 0))

        dps = [mm(values[h, j, at], backs[h], (1, 0)) for h, at in pieces]
        for (h, at), dp in zip(pieces, dps):
            finish(h, at, dp)
        return tuple(new)

    dquery = lax.fori_loop(0, block + 1, pull, tuple(jnp.zeros((HEAD, TILE), F32) for _ in every))
    for h in every:
        dq = dquery[h] * (1.0 / math.sqrt(HEAD))
        back_ref[turn_at * fused + h, block] = turn(dq, cos_ref[block], -sin_ref[block]).astype(BF)

    @pl.when(step == steps - 1)
    def _():
        @pl.loop(0, tiles)
        def _(j):
            for h in every:
                at = heads + turn_at * fused + h
                back_ref[at, j] = turn(dkeys[h, j].T, cos_ref[j], -sin_ref[j]).astype(BF)
                back_ref[heads + at, j] = dvalues[h, j].T.astype(BF)


def attend(place, qkv, cosine, sine, owners, sharers):
    parts, tiles, _, _ = qkv.shape
    heads = parts // 4
    held = (place.shape[0] - 1) // owners
    steps = tiles // sharers
    fused = heads if tiles <= 16 else 1
    turns = heads // fused

    def share(step, place_ref):
        return 2 * sharers * (step // 2) + jnp.where(step % 2 == 0, place_ref[0], 2 * sharers - 1 - place_ref[0])

    all_tiles, one_tile = (fused, tiles, HEAD, TILE), (fused, 1, HEAD, TILE)
    return pl.pallas_call(
        functools.partial(attention_kernel, share, fused, held),
        grid_spec=pltpu.PrefetchScalarGridSpec(
            num_scalar_prefetch=1,
            grid=(turns, steps),
            in_specs=[
                pl.BlockSpec(one_tile, lambda h, n, p: (h, share(n, p), 0, 0)),
                pl.BlockSpec(all_tiles, lambda h, n, p: (turns + h, 0, 0, 0)),
                pl.BlockSpec(all_tiles, lambda h, n, p: (2 * turns + h, 0, 0, 0)),
                pl.BlockSpec(one_tile, lambda h, n, p: (3 * turns + h, share(n, p), 0, 0)),
                whole((tiles, HALF, TILE)),
                whole((tiles, HALF, TILE)),
            ],
            out_specs=[whole((owners, heads, held, HEAD, RUN)), whole((3 * heads, tiles, HEAD, TILE))],
            scratch_shapes=[
                pltpu.VMEM((fused, tiles, TILE, HEAD), BF),
                pltpu.VMEM((fused, tiles, TILE, HEAD), BF),
                pltpu.VMEM((fused, tiles, TILE, HEAD), F32),
                pltpu.VMEM((fused, tiles, TILE, HEAD), F32),
                pltpu.VMEM((fused, tiles, TILE, TILE), F32),
                pltpu.VMEM((fused, tiles, TILE, TILE), BF),
            ],
        ),
        out_shape=[jax.ShapeDtypeStruct((owners, heads, held, HEAD, RUN), BF),
                   jax.ShapeDtypeStruct((3 * heads, tiles, HEAD, TILE), BF)],
        compiler_params=pltpu.CompilerParams(vmem_limit_bytes=VMEM_LIMIT),
        cost_estimate=cost(40 * heads * HEAD * tiles * TILE * steps * TILE, 4 * qkv.size),
        name="attend",
    )(place, qkv, qkv, qkv, qkv, cosine, sine)


def back_weight_kernel(order_ref, b_ref, w_ref, xa_ref, xb_ref, ga_ref, gb_ref, ma_ref, mb_ref, gain_ref, shift_ref,
                       _, __, dw_ref, dout_ref, dbias_ref, dgain_ref, dshift_ref, acc):
    step = pl.program_id(0)

    @pl.when(step == 0)
    def _():
        acc[...] = jnp.zeros_like(acc)
        dout_ref[...] = jnp.zeros_like(dout_ref)
        dbias_ref[...] = jnp.zeros_like(dbias_ref)

    xhat, _ = normalize(jnp.concatenate([xa_ref[0], xb_ref[0]], 0).astype(F32))
    rows, cols = b_ref.shape[0] * HEAD, ma_ref.shape[1] * HEAD
    back = b_ref[...].reshape(rows, TILE)
    acc[...] += mm(back, xhat.astype(BF), (1, 0))
    mixed = jnp.concatenate([r[0, :, 0].reshape(cols, RUN) for r in (ma_ref, mb_ref)], 1)
    dout_ref[...] += mm(mixed, jnp.concatenate([ga_ref[0], gb_ref[0]], 0), (1, 0))
    dbias_ref[...] += jnp.sum(back.astype(F32), 1, keepdims=True)

    @pl.when(step == pl.num_programs(0) - 1)
    def _():
        weight = w_ref[...].astype(F32)
        bias = dbias_ref[...]
        dgain_ref[...] = jnp.sum(acc[...] * weight, 0, keepdims=True)
        dshift_ref[...] = jnp.sum(bias * weight, 0, keepdims=True)
        dw_ref[...] = (acc[...] * gain_ref[...] + bias * shift_ref[...]).T.astype(BF)


def back_input_kernel(order_ref, b_ref, w_ref, gain_ref, _, __, e_ref):
    step = pl.program_id(0)
    back = b_ref[...].reshape(b_ref.shape[0] * HEAD, TILE)
    e = (mm(back, w_ref[...], (0, 0)) * gain_ref[...]).astype(BF)
    e_ref[order_ref[2 * step]] = e[:RUN]
    e_ref[order_ref[2 * step + 1]] = e[RUN:]


def back_to_weight(order, back, w, both_all, mixed, gain, shift, earlier):
    owners, _, width = both_all.shape
    held = order.shape[0] // owners
    rows = w.shape[0]
    parts, tiles, _, _ = back.shape
    heads = parts // 3
    line = jax.ShapeDtypeStruct((1, width), F32)

    def mixed_at(i, order, k):
        run = order[2 * i + k]
        return run // held, 0, run % held, 0, 0

    mixed_specs = [pl.BlockSpec((1, heads, 1, HEAD, RUN), lambda i, order, k=k: mixed_at(i, order, k)) for k in (0, 1)]
    return pl.pallas_call(
        back_weight_kernel,
        grid_spec=pltpu.PrefetchScalarGridSpec(
            num_scalar_prefetch=1,
            grid=(tiles,),
            in_specs=[pl.BlockSpec((parts, 1, HEAD, TILE), lambda i, order: (0, i, 0, 0)), whole((rows, width))]
            + run_specs(width, held, 0) + run_specs(width, held, held) + mixed_specs
            + [whole((1, width)), whole((1, width)), ANY, ANY],
            out_specs=[whole((width, rows)), whole((heads * HEAD, width)), whole((rows, 1)), whole((1, width)),
                       whole((1, width))],
            scratch_shapes=[pltpu.VMEM((rows, width), F32)],
        ),
        out_shape=[jax.ShapeDtypeStruct((width, rows), BF), jax.ShapeDtypeStruct((heads * HEAD, width), F32),
                   jax.ShapeDtypeStruct((rows, 1), F32), line, line],
        compiler_params=pltpu.CompilerParams(vmem_limit_bytes=VMEM_LIMIT),
        cost_estimate=cost(5 * tiles * TILE * width * rows, 4 * both_all.size),
        name="back_to_weight",
    )(order, back, w, both_all, both_all, both_all, both_all, mixed, mixed, gain, shift, *earlier)


def back_to_input(order, back, w, gain, earlier):
    rows, width = w.shape
    parts, tiles, _, _ = back.shape
    runs = order.shape[0]
    return pl.pallas_call(
        back_input_kernel,
        grid_spec=pltpu.PrefetchScalarGridSpec(
            num_scalar_prefetch=1,
            grid=(tiles,),
            in_specs=[pl.BlockSpec((parts, 1, HEAD, TILE), lambda i, order: (0, i, 0, 0)), whole((rows, width)),
                      whole((1, width)), ANY, ANY],
            out_specs=whole((runs, RUN, width)),
        ),
        out_shape=jax.ShapeDtypeStruct((runs, RUN, width), BF),
        compiler_params=pltpu.CompilerParams(vmem_limit_bytes=VMEM_LIMIT),
        cost_estimate=cost(5 * tiles * TILE * width * rows, 8 * back.size),
        name="back_to_input",
    )(order, back, w, gain, *earlier)


def ff_place_kernel(at_ref, all_ref, up_ref, down_ref):
    step_rows, shards = up_ref.shape[0], up_ref.shape[1] // all_ref.shape[2]
    hidden = all_ref.shape[2]
    value = all_ref[0].astype(F32)
    for k in range(shards):
        at = pl.multiple_of((at_ref[0] ^ k) * hidden, hidden)
        up_ref[:, pl.ds(at, hidden)] = value[k * step_rows:(k + 1) * step_rows]
    down_ref[...] = value[shards * step_rows:]


def place_ff(at, gathered, shards, step_rows):
    owners, rows, width = gathered.shape
    down_rows = rows - shards * step_rows
    return pl.pallas_call(
        ff_place_kernel,
        grid_spec=pltpu.PrefetchScalarGridSpec(
            num_scalar_prefetch=1,
            grid=(owners,),
            in_specs=[pl.BlockSpec((1, rows, width), lambda i, at: (i, 0, 0))],
        out_specs=[pl.BlockSpec((step_rows, shards * width), lambda i, core: (i, 0)),
                       pl.BlockSpec((down_rows, width), lambda i, core: (i, 0))],
        ),
        out_shape=[jax.ShapeDtypeStruct((owners * step_rows, shards * width), F32),
                   jax.ShapeDtypeStruct((owners * down_rows, width), F32)],
        compiler_params=pltpu.CompilerParams(vmem_limit_bytes=VMEM_LIMIT),
        name="place_ff",
    )(at, gathered)


def io_place_kernel(cols, core_ref, mine_ref, other_ref, in_ref, out_ref, line_ref):
    parity = pl.program_id(0)
    own = parity == core_ref[0]
    count, rows, width = mine_ref.shape
    half = rows // 2
    groups = width // cols
    held = count // groups
    for g in range(groups):
        value = None
        for i in range(held):
            at = g * held + i
            one = jnp.where(own, mine_ref[at].astype(F32), other_ref[at].astype(F32))
            value = one if value is None else value + one
        for part in range(3):
            at = part * width + g * cols
            in_ref[:, at:at + cols] = value[half:, part * cols:(part + 1) * cols]
        if g == 0:
            out_ref[...] = value[:half]
            line_ref[...] = value[half:, 3 * cols:]
        else:
            out_ref[...] += value[:half]
            line_ref[...] += value[half:, 3 * cols:]


def place_io(core, mine, other, cols):
    count, rows, width = mine.shape
    half = rows // 2
    return pl.pallas_call(
        functools.partial(io_place_kernel, cols),
        grid_spec=pltpu.PrefetchScalarGridSpec(
            num_scalar_prefetch=1,
            grid=(2,),
            in_specs=[whole(mine.shape), whole(other.shape)],
            out_specs=[pl.BlockSpec((half, 3 * width), lambda i, core: (i, 0)),
                       pl.BlockSpec((half, width), lambda i, core: (i, 0)),
                       pl.BlockSpec((half, width - 3 * cols), lambda i, core: (i, 0))],
        ),
        out_shape=[jax.ShapeDtypeStruct((rows, 3 * width), F32), jax.ShapeDtypeStruct((rows, width), F32),
                   jax.ShapeDtypeStruct((rows, width - 3 * cols), F32)],
        compiler_params=pltpu.CompilerParams(vmem_limit_bytes=VMEM_LIMIT),
        name="place_io",
    )(core[None], mine, other)


def spread_out(pieces, axis, groups=None):
    return lax.all_to_all(pieces, axis, 0, 0, axis_index_groups=groups)


def to_all_value(x, count):
    return jnp.broadcast_to(x[None], (count,) + x.shape)


def to_all(x, axis, groups=None, count=None):
    return spread_out(to_all_value(x, count or lax.axis_size(axis)), axis, groups)


def at_distance(pieces):
    count = len(pieces)
    return [pieces[0]] + [
        lax.ppermute(pieces[k], "fsdp", [(i, i ^ k) for i in range(count)]) for k in range(1, count)]


def by_distance(pieces, shard):
    return at_distance([
        lax.dynamic_index_in_dim(pieces, shard ^ k, 0, keepdims=False) for k in range(pieces.shape[0])])


def total(values):
    result = values[0].astype(F32)
    for v in values[1:]:
        result = result + v.astype(F32)
    return result


def after(index, value):
    first = value[(0,) * value.ndim]
    return index + (first != first).astype(jnp.int32)


def on_device(
    inputs, positions, in_weight, in_bias, out_weight, out_bias, up_weight, up_bias, down_weight, down_bias,
    first_gain, first_shift, second_gain, second_shift, out_grad,
):
    x, grad, place = inputs[0], out_grad[0], positions[0]
    tokens, width = x.shape
    owners, shards = lax.axis_size("ctx"), lax.axis_size("fsdp")
    here, shard = lax.axis_index("ctx"), lax.axis_index("fsdp")
    heads = width // HEAD
    groups = math.gcd(heads, owners // 2)
    sharers = owners // groups
    own_heads = heads // groups
    cols = own_heads * HEAD
    group, sharer, core = here // sharers, here % sharers, here % 2
    hidden = down_weight.shape[0]
    rows = in_weight.shape[0]
    half = rows // 2
    length = tokens * owners
    held = tokens // RUN
    joined = hidden == width
    tiles = length // TILE
    parity = [[i for i in range(owners) if i % 2 == k] for k in (0, 1)]
    pairs = [(i, i ^ 1) for i in range(owners)]

    def swap(value):
        return lax.ppermute(value, "ctx", pairs)

    def both(mine, other):
        return jnp.stack([jnp.where(core == 0, mine, other), jnp.where(core == 0, other, mine)], 1)

    run_rows = jnp.broadcast_to(jnp.pad((place[::RUN] // RUN).astype(BF), (0, width - held))[None], (16, width))
    both_all = lax.all_gather(jnp.concatenate([x, grad, run_rows], 0), "ctx", axis=0, tiled=False)

    def block(values):
        lines = [jnp.pad(v[None], ((0, 0), (0, width - v.shape[0]))) for v in values]
        return jnp.pad(jnp.concatenate(lines, 0), ((0, 16 - len(values)), (0, 0)))

    small_block = block([second_gain, second_shift])
    smalls = [in_bias, out_bias, down_bias, first_gain, first_shift]

    def own_half(value, at=core):
        return lax.dynamic_slice_in_dim(value, at * half, half, 0)

    up_pieces = own_half(up_weight).reshape(half, shards, hidden).transpose(1, 0, 2)
    shared = to_all_value(jnp.concatenate([x, grad, small_block], 0), shards)
    skip = -(-(2 * tokens + 16) // (half // 2)) * (half // 2)
    if joined:
        gap = jnp.zeros((shards, skip - 2 * tokens - 16, width), BF)
        plane = spread_out(jnp.concatenate([shared, gap, up_pieces], 1), "fsdp")
        up_own = plane[:, skip:]
    else:
        plane, up_own = spread_out(shared, "fsdp"), spread_out(up_pieces, "fsdp")
    later = after(core, plane)
    in_own = own_half(in_weight, later).reshape(half, 3, groups, cols)
    in_own = lax.dynamic_index_in_dim(in_own, group, 2, keepdims=False).reshape(half, 3 * cols)
    in_own = jnp.pad(in_own, ((0, 0), (0, width - 3 * cols)))
    io_send = to_all_value(jnp.concatenate([own_half(out_weight, later), in_own, block(smalls)], 0), shards)
    io_got = spread_out(io_send, "fsdp")
    small_got, io_got = io_got[:, 2 * half:].astype(F32), io_got[:, :2 * half]

    full_in_bias, full_out_bias, full_down_bias, gain_one, shift_one = [
        small_got[:, i, :s.shape[0]].reshape(-1) for i, s in enumerate(smalls)]

    small_step = rows // owners
    packed = joined and small_step % 8 == 0
    up_other, up_bias_row = swap(up_own), up_bias.astype(F32)[None]
    *ff_parts, up_part, down_part, up_bias_part, gain_two_part, shift_two_part = feed_forward(
        jnp.stack([core, shard]), plane, tokens, plane if joined else up_own, up_other, skip, down_weight,
        up_bias_row, owners if packed else 0)

    def give_half(pieces, axis, mine=core):
        keep = lax.dynamic_index_in_dim(pieces, mine, axis, keepdims=False)
        give = lax.dynamic_index_in_dim(pieces, 1 - mine, axis, keepdims=False)
        return (keep.astype(F32) + swap(give).astype(F32)).astype(BF)

    def reduce_owners(pieces):
        return lax.psum_scatter(pieces, "ctx", scatter_dimension=0, tiled=False)

    def gather_owners(value):
        mine = to_all(value, "ctx", parity, owners // 2)
        return mine, swap(mine)

    cut = shards * small_step
    if packed:
        summed = reduce_owners(up_part + after(jnp.int32(0), both_all).astype(BF))
        up_sum, down_sum = summed[:cut], summed[cut:]
    else:
        up_pieces = up_part.reshape(shards, owners, small_step, hidden).transpose(1, 0, 2, 3)
        up_sum = reduce_owners(up_pieces.reshape(owners, cut, hidden))
        down_sum = reduce_owners(down_part.reshape(owners, hidden // owners, width))

    io_got = io_got + after(jnp.int32(0), ff_parts[0]).astype(BF)
    io_full = both(io_got, swap(io_got)).reshape(shards, 2, 2, half, width)
    out_full = io_full[:, :, 0].reshape(width, width)
    in_full = io_full[:, :, 1].reshape(width, width)[:, :3 * cols].T
    out_own = lax.dynamic_slice_in_dim(out_full, group * cols, cols, 0)
    run_at = both_all[:, 2 * tokens, :held].reshape(-1).astype(jnp.int32)
    runs = run_at.shape[0]
    at_run = lax.broadcasted_iota(jnp.int32, (runs, runs), 0)
    of_run = lax.broadcasted_iota(jnp.int32, (runs, runs), 1)
    order = jnp.sum(jnp.where(run_at[None] == at_run, of_run, 0), 1)

    ladder = 10000.0 ** (-jnp.arange(0, ROT, 2, dtype=F32) / ROT)
    angle = jnp.arange(length, dtype=jnp.int32).astype(F32).reshape(tiles, 1, TILE) * ladder[None, :, None]
    cosine, sine = jnp.cos(angle), jnp.sin(angle)

    bias_own = lax.dynamic_index_in_dim(full_in_bias.reshape(3, groups, cols), group, 1, keepdims=False)
    qkv = project(order, both_all, in_full, out_own, bias_own.reshape(-1, 1), gain_one[None], shift_one[None],
                  cosine, sine)
    spots = jnp.concatenate([sharer[None].astype(jnp.int32), order])
    ff_got = at_distance(ff_parts)
    mixed_out, back_qkv = attend(spots, qkv, cosine, sine, owners, sharers)
    up_sum = jnp.concatenate(by_distance(up_sum.reshape(shards, small_step, hidden), after(shard, back_qkv)), 0)
    mixed_own = give_half(mixed_out.reshape(owners // 2, 2, own_heads, held, HEAD, RUN), 1)
    mixed_got = spread_out(mixed_own, "ctx", parity)
    if joined:
        ff_own = jnp.concatenate([up_sum, down_sum], 0)
        ff_all = lax.all_gather(ff_own, "ctx", axis=0, tiled=False)
        up_all, down_all = ff_all[:, :cut], ff_all[:, cut:]
    else:
        ff_own = up_sum
        up_all, down_all = [lax.all_gather(v, "ctx", axis=0, tiled=False) for v in (up_sum, down_sum)]
    x32, grad32 = x.astype(F32), grad.astype(F32)
    gain_row, shift_row = gain_one[None], shift_one[None]
    in_part, out_part, in_bias_part, gain_one_part, shift_one_part = back_to_weight(
        order, back_qkv, in_full, both_all, mixed_out, gain_row, shift_row, (mixed_own, ff_own))
    if packed:
        up_weight_gradient, down_weight_gradient = place_ff(shard[None], ff_all, shards, small_step)
    else:
        up_all = up_all.reshape(owners, shards, small_step, hidden)
        up_all = [lax.dynamic_index_in_dim(up_all, shard ^ f, 1, keepdims=False) for f in range(shards)]
        up_weight_gradient = jnp.concatenate(up_all, -1).reshape(rows, shards * hidden).astype(F32)
        down_weight_gradient = down_all.reshape(hidden, width).astype(F32)

    mixed_got = mixed_got + after(jnp.int32(0), in_part).astype(BF)
    ff_sum = total(ff_got) + after(jnp.int32(0), down_weight_gradient).astype(F32)
    mixed = jnp.sum(mixed_got.astype(F32).reshape(groups, sharers // 2, own_heads, held, HEAD, RUN), 1)
    mixed = mixed.transpose(0, 1, 3, 2, 4).reshape(width, tokens).astype(BF)
    branch = mm(mixed, out_full, (0, 0))
    output = x32 + (branch + full_out_bias) + (ff_sum[:tokens] + full_down_bias)

    in_bias_full = lax.dynamic_update_slice_in_dim(
        jnp.zeros((3, groups, cols), F32), in_bias_part.reshape(3, 1, cols), group, 1)
    lines = [in_bias_full.reshape(-1), jnp.sum(grad32, 0), gain_one_part[0], shift_one_part[0], gain_two_part[0],
             shift_two_part[0]]
    lines = [v.reshape(shards, -1) for v in lines]
    at_shard = (jnp.arange(shards) == shard)[:, None]
    lines.append(jnp.where(at_shard, up_bias_part, 0.0))
    line_sizes = [v.shape[1] for v in lines]
    lines = jnp.concatenate(lines, 1).astype(BF).reshape(shards, 2, -1, width - 3 * cols)
    line_rows = lines.shape[2]
    lines = jnp.pad(lines, ((0, 0), (0, 0), (0, half - line_rows), (0, 0)))
    out_rows = lax.dynamic_update_slice_in_dim(
        jnp.zeros((width, width), BF), out_part.astype(BF), group * cols, 0)
    in_pieces = jnp.concatenate([in_part.reshape(shards, 2, half, 3 * cols), lines], 3)
    pieces = jnp.concatenate([out_rows.reshape(shards, 2, half, width), in_pieces], 2)
    pieces = give_half(pieces, 1, after(core, mixed_got))
    e_runs = back_to_input(order, back_qkv, in_full, gain_row, (pieces, pieces))
    e_sum = lax.psum_scatter(e_runs.reshape(length, width), "ctx", scatter_dimension=0, tiled=True)
    pieces = total(by_distance(pieces, shard)).astype(BF)
    pieces = pieces + after(jnp.int32(0), down_weight_gradient).astype(BF)
    in_weight_gradient, out_weight_gradient, line_sum = place_io(
        core, *gather_owners(pieces), cols)
    line_sum = line_sum.reshape(2, half, -1)[:, :line_rows].reshape(-1)
    totals, at = [], 0
    for size in line_sizes:
        totals.append(line_sum[at:at + size])
        at += size

    e = e_sum.astype(F32) + ff_sum[tokens:]
    xhat, inverse = normalize(x32)
    input_gradient = grad32 + inverse * (
        e - jnp.mean(e, -1, keepdims=True) - xhat * jnp.mean(e * xhat, -1, keepdims=True))
    return (
        output.astype(BF)[None], input_gradient[None], in_weight_gradient, totals[0], out_weight_gradient, totals[1],
        up_weight_gradient, totals[6], down_weight_gradient, totals[1], totals[2], totals[3], totals[4], totals[5],
    )


def solution(mesh):
    token, matrix, vector = P("fsdp", "ctx", None), P("fsdp", None), P("fsdp")
    return jax.shard_map(
        on_device,
        mesh=mesh,
        in_specs=(token, P("fsdp", "ctx"), matrix, vector, matrix, vector, matrix, vector, matrix, vector,
                  vector, vector, vector, vector, token),
        out_specs=(token, token, matrix, vector, matrix, vector, matrix, vector, matrix, vector,
                   vector, vector, vector, vector),
        check_vma=False,
    )
```

```python
import functools
import math

import jax
import jax.numpy as jnp
from jax import lax
from jax.experimental import pallas as pl
from jax.experimental.pallas import tpu as pltpu
from jax.sharding import PartitionSpec as P

HEAD = 64
ROT = 16
HALF = ROT // 2
RUN = 128
TILE = 256
SUB = 256
NEG = -1e30
EPS = 1e-05
BF = jnp.bfloat16
F32 = jnp.float32
VMEM_LIMIT = 60 * 1024 * 1024


def mm(left, right, dims):
    return lax.dot_general(left, right, ((dims[:1], dims[1:]), ((), ())), preferred_element_type=F32)


def flip(x):
    return x.astype(F32).T.astype(x.dtype)


def normalize(values):
    mean = jnp.mean(values, -1, keepdims=True)
    centred = values - mean
    spread = jnp.mean(centred * centred, -1, keepdims=True)
    inverse = lax.rsqrt(spread + EPS)
    return centred * inverse, inverse


def turn(values, cosine, sine):
    one, two = values[:HALF], values[HALF:ROT]
    return jnp.concatenate([one * cosine - two * sine, two * cosine + one * sine, values[ROT:]], 0)


def ff_kernel(packed, core_ref, x_ref, g_ref, small_ref, mine_ref, mine_end_ref, other_ref, down_ref, upb_ref,
              *refs):
    shards = small_ref.shape[0]
    outs, refs = refs[:shards], refs[shards:]
    (dup_ref, ddown_ref, dbias_ref, dgain_ref, dshift_ref, acc_up, acc_down, up_ref, gain_ref, shift_ref) = refs
    step = pl.program_id(0)

    @pl.when(step == 0)
    def _():
        half = other_ref.shape[1]
        share = gain_ref.shape[1] // shards
        first = core_ref[0] == 0
        for f in range(shards):
            mine = jnp.concatenate([mine_ref[f].astype(F32), mine_end_ref[f].astype(F32)], 0)
            other = other_ref[f].astype(F32)
            at = 2 * f * half
            up_ref[at:at + half] = jnp.where(first, mine, other).astype(BF)
            up_ref[at + half:at + 2 * half] = jnp.where(first, other, mine).astype(BF)
            small = small_ref[f].astype(F32)
            gain_ref[:, f * share:(f + 1) * share] = small[0:1, :share]
            shift_ref[:, f * share:(f + 1) * share] = small[1:2, :share]
        acc_up[...] = jnp.zeros_like(acc_up)
        acc_down[...] = jnp.zeros_like(acc_down)
        dbias_ref[...] = jnp.zeros_like(dbias_ref)
        dgain_ref[...] = jnp.zeros_like(dgain_ref)
        dshift_ref[...] = jnp.zeros_like(dshift_ref)

    grad = g_ref[0]
    back_active = mm(grad, down_ref[...], (1, 1))
    xhat, _ = normalize(x_ref[0].astype(F32))
    second = (xhat * gain_ref[...] + shift_ref[...]).astype(BF)
    up = mm(second, up_ref[...], (1, 0)) + upb_ref[...]
    phi = 0.5 * (1.0 + lax.erf(up * (1.0 / math.sqrt(2.0))))
    active = (up * phi).astype(BF)
    slope = phi + up * jnp.exp(-0.5 * up * up) * (1.0 / math.sqrt(2.0 * math.pi))
    tokens = x_ref.shape[1]
    part = mm(active, down_ref[...], (1, 0)).astype(BF)
    low_up = (back_active * slope).astype(BF)
    dbias_ref[...] += jnp.sum(low_up.astype(F32), 0, keepdims=True)
    acc_up[...] += mm(second, low_up, (0, 0))
    acc_down[...] += mm(active, grad, (0, 0))
    back = mm(low_up, up_ref[...], (1, 1))
    dgain_ref[...] += jnp.sum(back * xhat, 0, keepdims=True)
    dshift_ref[...] += jnp.sum(back, 0, keepdims=True)
    back = (back * gain_ref[...]).astype(BF)
    for k in range(shards):
        @pl.when(step == k)
        def _(k=k):
            outs[k][:tokens] = part
            outs[k][tokens:] = back

    @pl.when(step == pl.num_programs(0) - 1)
    def _():
        if packed:
            owners = dup_ref.shape[0]
            rows = acc_up.shape[0] // shards
            few = rows // owners
            down_rows = acc_down.shape[0] // owners
            for c in range(owners):
                up_rows = [acc_up[f * rows + c * few:f * rows + (c + 1) * few] for f in range(shards)]
                dup_ref[c] = jnp.concatenate(
                    up_rows + [acc_down[c * down_rows:(c + 1) * down_rows]], 0).astype(BF)
            ddown_ref[...] = jnp.zeros_like(ddown_ref)
        else:
            dup_ref[...] = acc_up[...].astype(BF)
            ddown_ref[...] = acc_down[...].astype(BF)


ANY = pl.BlockSpec(memory_space=pl.ANY)


def whole(shape):
    return pl.BlockSpec(shape, lambda *_: (0,) * len(shape))


def cost(macs, size):
    return pl.CostEstimate(flops=int(2 * macs), bytes_accessed=int(size), transcendentals=0)


def feed_forward(at, got, tokens, up_mine, up_other, skip, down, up_bias, owners):
    groups, _, width = got.shape
    hidden = down.shape[0]
    half = width // groups // 2
    quarter = half // 2
    at_up = skip // quarter if up_mine is got else 0
    x_tile = pl.BlockSpec((1, tokens, width), lambda i, at: (at[1] ^ i, 0, 0))
    g_tile = pl.BlockSpec((1, tokens, width), lambda i, at: (at[1] ^ i, 1, 0))
    small_tile = pl.BlockSpec((groups, 16, width), lambda i, at: (0, 2 * tokens // 16, 0))
    row = jax.ShapeDtypeStruct((1, width), F32)
    if owners:
        shapes = [(owners, (width + hidden) // owners, hidden), (16, 128)]
    else:
        shapes = [(width, hidden), (hidden, width)]
    return pl.pallas_call(
        functools.partial(ff_kernel, bool(owners)),
        grid_spec=pltpu.PrefetchScalarGridSpec(
            num_scalar_prefetch=1,
            grid=(groups,),
            in_specs=[x_tile, g_tile, small_tile,
                      pl.BlockSpec((groups, quarter, hidden), lambda i, at: (0, at_up, 0)),
                      pl.BlockSpec((groups, quarter, hidden), lambda i, at: (0, at_up + 1, 0)),
                      whole((groups, half, hidden)), whole((hidden, width)), whole((1, hidden))],
            out_specs=[whole((2 * tokens, width))] * groups + [whole(shape) for shape in shapes]
            + [whole((1, hidden)), whole((1, width)), whole((1, width))],
            scratch_shapes=[pltpu.VMEM((width, hidden), F32), pltpu.VMEM((hidden, width), F32),
                            pltpu.VMEM((width, hidden), BF), pltpu.VMEM((1, width), F32),
                            pltpu.VMEM((1, width), F32)],
        ),
        out_shape=[jax.ShapeDtypeStruct((2 * tokens, width), BF)] * groups
        + [jax.ShapeDtypeStruct(shape, BF) for shape in shapes]
        + [jax.ShapeDtypeStruct((1, hidden), F32), row, row],
        compiler_params=pltpu.CompilerParams(vmem_limit_bytes=VMEM_LIMIT),
        cost_estimate=cost(12 * groups * tokens * width * hidden, 4 * got.size),
        name="feed_forward",
    )(at, got, got, got, up_mine, up_mine, up_other, down, up_bias)


def qkv_kernel(order_ref, xa_ref, xb_ref, ga_ref, gb_ref, w_ref, wo_ref, bias_ref, gain_ref, shift_ref, cos_ref,
               sin_ref, out_ref):
    back = mm(wo_ref[...], jnp.concatenate([ga_ref[0], gb_ref[0]], 0), (1, 1)).astype(BF)
    values = jnp.concatenate([xa_ref[0], xb_ref[0]], 0).astype(F32)
    xhat, _ = normalize(values)
    first = (xhat * gain_ref[...] + shift_ref[...]).astype(BF)
    proj = mm(w_ref[...], first, (1, 1)) + bias_ref[...]
    heads = out_ref.shape[0] // 4
    cosine, sine = cos_ref[0], sin_ref[0]
    for i in range(3 * heads):
        part = proj[i * HEAD:(i + 1) * HEAD]
        if i < 2 * heads:
            part = turn(part, cosine, sine)
        part = part.astype(BF)
        if i < heads:
            part = part * jnp.asarray(1.0 / math.sqrt(HEAD), BF)
        out_ref[i, 0] = part
    for i in range(heads):
        out_ref[3 * heads + i, 0] = back[i * HEAD:(i + 1) * HEAD]


def run_specs(width, held, skip):
    def at(i, order, k):
        run = order[2 * i + k]
        return run // held, run % held + skip, 0

    return [pl.BlockSpec((1, RUN, width), lambda i, order, k=k: at(i, order, k)) for k in (0, 1)]


def project(order, both_all, w, w_out, bias, gain, shift, cosine, sine):
    owners, _, width = both_all.shape
    held = order.shape[0] // owners
    rows, cols = w.shape[0], w_out.shape[0]
    tiles = order.shape[0] // 2
    parts = (rows + cols) // HEAD
    table = pl.BlockSpec((1, HALF, TILE), lambda i, order: (i, 0, 0))
    return pl.pallas_call(
        qkv_kernel,
        grid_spec=pltpu.PrefetchScalarGridSpec(
            num_scalar_prefetch=1,
            grid=(tiles,),
            in_specs=run_specs(width, held, 0) + run_specs(width, held, held)
            + [whole((rows, width)), whole((cols, width)), whole((rows, 1)), whole((1, width)),
               whole((1, width)), table, table],
            out_specs=pl.BlockSpec((parts, 1, HEAD, TILE), lambda i, order: (0, i, 0, 0)),
        ),
        out_shape=jax.ShapeDtypeStruct((parts, tiles, HEAD, TILE), BF),
        compiler_params=pltpu.CompilerParams(vmem_limit_bytes=VMEM_LIMIT),
        cost_estimate=cost(5 * tiles * TILE * width * (rows + cols), 4 * both_all.size),
        name="project",
    )(order, both_all, both_all, both_all, both_all, w, w_out, bias, gain, shift, cosine, sine)


def attention_kernel(share, fused, held, place_ref, q_ref, k_ref, v_ref, d_ref, cos_ref, sin_ref,
                     mix_ref, back_ref, keys, values, dkeys, dvalues, sbuf, pbuf):
    turn_at, step = pl.program_id(0), pl.program_id(1)
    heads, steps = pl.num_programs(0) * fused, pl.num_programs(1)
    tiles = k_ref.shape[1]
    block = share(step, place_ref)
    every = range(fused)

    @pl.when((turn_at == 0) & (step == 0))
    def _():
        mix_ref[...] = jnp.zeros_like(mix_ref)
        queries_end = back_ref.shape[0] // 3
        back_ref[:queries_end] = jnp.zeros((queries_end,) + back_ref.shape[1:], BF)

    @pl.when(step == 0)
    def _():
        @pl.loop(0, tiles)
        def _(j):
            for h in every:
                keys[h, j] = flip(k_ref[h, j])
                values[h, j] = flip(v_ref[h, j])
                dkeys[h, j] = jnp.zeros((TILE, HEAD), F32)
                dvalues[h, j] = jnp.zeros((TILE, HEAD), F32)

    queries = [q_ref[h, 0] for h in every]

    def fold(x, op):
        return op(x.reshape(x.shape[0] // 8, 8, TILE), 0)

    pieces = [(h, slice(i, i + SUB)) for h in every for i in range(0, TILE, SUB)]

    def score(j, peaks):
        new = list(peaks)
        for h, at in pieces:
            s = mm(keys[h, j, at], queries[h], (1, 0))
            sbuf[h, j, at] = s
            new[h] = jnp.maximum(new[h], fold(s, jnp.max))
        return tuple(new)

    peaks = lax.fori_loop(0, block, score, tuple(jnp.full((8, TILE), NEG, F32) for _ in every))
    key_at = lax.broadcasted_iota(jnp.int32, (TILE, TILE), 0)
    query_at = lax.broadcasted_iota(jnp.int32, (TILE, TILE), 1)
    last = []
    for h in every:
        s = jnp.where(key_at <= query_at, mm(keys[h, block], queries[h], (1, 0)), NEG)
        sbuf[h, block] = s
        last.append(jnp.max(jnp.maximum(peaks[h], fold(s, jnp.max)), 0, keepdims=True))
    peaks = last

    def weigh(j, carry):
        new = list(carry)
        for h, at in pieces:
            total, mixed = new[h]
            p = jnp.exp(sbuf[h, j, at] - peaks[h])
            low = p.astype(BF)
            pbuf[h, j, at] = low
            new[h] = (total + fold(p, jnp.sum), mixed)
        for h, at in pieces:
            total, mixed = new[h]
            new[h] = (total, mixed + mm(v_ref[h, j, :, at], pbuf[h, j, at], (1, 0)))
        return tuple(new)

    sums = lax.fori_loop(
        0, block + 1, weigh,
        tuple((jnp.zeros((8, TILE), F32), jnp.zeros((HEAD, TILE), F32)) for _ in every))
    spreads, backs, back_rows, query_rows = [], [], [], []
    for h in every:
        total, mixed = sums[h]
        inverse = 1.0 / jnp.sum(total, 0, keepdims=True)
        mixed = mixed * inverse
        low_mixed = mixed.astype(BF)
        for k in (0, 1):
            at = place_ref[1 + 2 * block + k]
            mix_ref[at // held, turn_at * fused + h, at % held] = low_mixed[:, k * RUN:(k + 1) * RUN]
        back = d_ref[h, 0].astype(F32) * inverse
        spreads.append(jnp.sum(back * mixed, 0, keepdims=True))
        back = back.astype(BF)
        backs.append(back)
        back_rows.append(flip(back))
        query_rows.append(flip(queries[h]))

    def pull(j, dquery):
        new = list(dquery)

        def finish(h, at, dp):
            low = pbuf[h, j, at]
            ds = (low.astype(F32) * (dp - spreads[h])).astype(BF)
            dvalues[h, j, at] += mm(low, back_rows[h], (1, 0))
            dkeys[h, j, at] += mm(ds, query_rows[h], (1, 0))
            new[h] = new[h] + mm(k_ref[h, j, :, at], ds, (1, 0))

        dps = [mm(values[h, j, at], backs[h], (1, 0)) for h, at in pieces]
        for (h, at), dp in zip(pieces, dps):
            finish(h, at, dp)
        return tuple(new)

    dquery = lax.fori_loop(0, block + 1, pull, tuple(jnp.zeros((HEAD, TILE), F32) for _ in every))
    for h in every:
        dq = dquery[h] * (1.0 / math.sqrt(HEAD))
        back_ref[turn_at * fused + h, block] = turn(dq, cos_ref[block], -sin_ref[block]).astype(BF)

    @pl.when(step == steps - 1)
    def _():
        @pl.loop(0, tiles)
        def _(j):
            for h in every:
                at = heads + turn_at * fused + h
                back_ref[at, j] = turn(dkeys[h, j].T, cos_ref[j], -sin_ref[j]).astype(BF)
                back_ref[heads + at, j] = dvalues[h, j].T.astype(BF)


def attend(place, qkv, cosine, sine, owners, sharers):
    parts, tiles, _, _ = qkv.shape
    heads = parts // 4
    held = (place.shape[0] - 1) // owners
    steps = tiles // sharers
    fused = heads if tiles <= 16 else 1
    turns = heads // fused

    def share(step, place_ref):
        return 2 * sharers * (step // 2) + jnp.where(step % 2 == 0, place_ref[0], 2 * sharers - 1 - place_ref[0])

    all_tiles, one_tile = (fused, tiles, HEAD, TILE), (fused, 1, HEAD, TILE)
    return pl.pallas_call(
        functools.partial(attention_kernel, share, fused, held),
        grid_spec=pltpu.PrefetchScalarGridSpec(
            num_scalar_prefetch=1,
            grid=(turns, steps),
            in_specs=[
                pl.BlockSpec(one_tile, lambda h, n, p: (h, share(n, p), 0, 0)),
                pl.BlockSpec(all_tiles, lambda h, n, p: (turns + h, 0, 0, 0)),
                pl.BlockSpec(all_tiles, lambda h, n, p: (2 * turns + h, 0, 0, 0)),
                pl.BlockSpec(one_tile, lambda h, n, p: (3 * turns + h, share(n, p), 0, 0)),
                whole((tiles, HALF, TILE)),
                whole((tiles, HALF, TILE)),
            ],
            out_specs=[whole((owners, heads, held, HEAD, RUN)), whole((3 * heads, tiles, HEAD, TILE))],
            scratch_shapes=[
                pltpu.VMEM((fused, tiles, TILE, HEAD), BF),
                pltpu.VMEM((fused, tiles, TILE, HEAD), BF),
                pltpu.VMEM((fused, tiles, TILE, HEAD), F32),
                pltpu.VMEM((fused, tiles, TILE, HEAD), F32),
                pltpu.VMEM((fused, tiles, TILE, TILE), F32),
                pltpu.VMEM((fused, tiles, TILE, TILE), BF),
            ],
        ),
        out_shape=[jax.ShapeDtypeStruct((owners, heads, held, HEAD, RUN), BF),
                   jax.ShapeDtypeStruct((3 * heads, tiles, HEAD, TILE), BF)],
        compiler_params=pltpu.CompilerParams(vmem_limit_bytes=VMEM_LIMIT),
        cost_estimate=cost(40 * heads * HEAD * tiles * TILE * steps * TILE, 4 * qkv.size),
        name="attend",
    )(place, qkv, qkv, qkv, qkv, cosine, sine)


def back_weight_kernel(order_ref, b_ref, w_ref, xa_ref, xb_ref, ga_ref, gb_ref, ma_ref, mb_ref, gain_ref, shift_ref,
                       _, __, dw_ref, dout_ref, dbias_ref, dgain_ref, dshift_ref, acc):
    step = pl.program_id(0)

    @pl.when(step == 0)
    def _():
        acc[...] = jnp.zeros_like(acc)
        dout_ref[...] = jnp.zeros_like(dout_ref)
        dbias_ref[...] = jnp.zeros_like(dbias_ref)

    rows, cols = b_ref.shape[0] * HEAD, ma_ref.shape[1] * HEAD
    mixed = jnp.concatenate([r[0, :, 0].reshape(cols, RUN) for r in (ma_ref, mb_ref)], 1)
    dout_ref[...] += mm(mixed, jnp.concatenate([ga_ref[0], gb_ref[0]], 0), (1, 0))
    xhat, _ = normalize(jnp.concatenate([xa_ref[0], xb_ref[0]], 0).astype(F32))
    back = b_ref[...].reshape(rows, TILE)
    acc[...] += mm(back, xhat.astype(BF), (1, 0))
    dbias_ref[...] += jnp.sum(back.astype(F32), 1, keepdims=True)

    @pl.when(step == pl.num_programs(0) - 1)
    def _():
        weight = w_ref[...].astype(F32)
        bias = dbias_ref[...]
        dgain_ref[...] = jnp.sum(acc[...] * weight, 0, keepdims=True)
        dshift_ref[...] = jnp.sum(bias * weight, 0, keepdims=True)
        dw_ref[...] = (acc[...] * gain_ref[...] + bias * shift_ref[...]).T.astype(BF)


def back_input_kernel(order_ref, b_ref, w_ref, gain_ref, _, __, e_ref):
    step = pl.program_id(0)
    back = b_ref[...].reshape(b_ref.shape[0] * HEAD, TILE)
    e = (mm(back, w_ref[...], (0, 0)) * gain_ref[...]).astype(BF)
    e_ref[order_ref[2 * step]] = e[:RUN]
    e_ref[order_ref[2 * step + 1]] = e[RUN:]


def back_to_weight(order, back, w, both_all, mixed, gain, shift, earlier):
    owners, _, width = both_all.shape
    held = order.shape[0] // owners
    rows = w.shape[0]
    parts, tiles, _, _ = back.shape
    heads = parts // 3
    line = jax.ShapeDtypeStruct((1, width), F32)

    def mixed_at(i, order, k):
        run = order[2 * i + k]
        return run // held, 0, run % held, 0, 0

    mixed_specs = [pl.BlockSpec((1, heads, 1, HEAD, RUN), lambda i, order, k=k: mixed_at(i, order, k)) for k in (0, 1)]
    return pl.pallas_call(
        back_weight_kernel,
        grid_spec=pltpu.PrefetchScalarGridSpec(
            num_scalar_prefetch=1,
            grid=(tiles,),
            in_specs=[pl.BlockSpec((parts, 1, HEAD, TILE), lambda i, order: (0, i, 0, 0)), whole((rows, width))]
            + run_specs(width, held, 0) + run_specs(width, held, held) + mixed_specs
            + [whole((1, width)), whole((1, width)), ANY, ANY],
            out_specs=[whole((width, rows)), whole((heads * HEAD, width)), whole((rows, 1)), whole((1, width)),
                       whole((1, width))],
            scratch_shapes=[pltpu.VMEM((rows, width), F32)],
        ),
        out_shape=[jax.ShapeDtypeStruct((width, rows), BF), jax.ShapeDtypeStruct((heads * HEAD, width), F32),
                   jax.ShapeDtypeStruct((rows, 1), F32), line, line],
        compiler_params=pltpu.CompilerParams(vmem_limit_bytes=VMEM_LIMIT),
        cost_estimate=cost(5 * tiles * TILE * width * rows, 4 * both_all.size),
        name="back_to_weight",
    )(order, back, w, both_all, both_all, both_all, both_all, mixed, mixed, gain, shift, *earlier)


def back_to_input(order, back, w, gain, earlier):
    rows, width = w.shape
    parts, tiles, _, _ = back.shape
    runs = order.shape[0]
    return pl.pallas_call(
        back_input_kernel,
        grid_spec=pltpu.PrefetchScalarGridSpec(
            num_scalar_prefetch=1,
            grid=(tiles,),
            in_specs=[pl.BlockSpec((parts, 1, HEAD, TILE), lambda i, order: (0, i, 0, 0)), whole((rows, width)),
                      whole((1, width)), ANY, ANY],
            out_specs=whole((runs, RUN, width)),
        ),
        out_shape=jax.ShapeDtypeStruct((runs, RUN, width), BF),
        compiler_params=pltpu.CompilerParams(vmem_limit_bytes=VMEM_LIMIT),
        cost_estimate=cost(5 * tiles * TILE * width * rows, 8 * back.size),
        name="back_to_input",
    )(order, back, w, gain, *earlier)


def ff_place_kernel(at_ref, all_ref, up_ref, down_ref):
    step_rows, shards = up_ref.shape[0], up_ref.shape[1] // all_ref.shape[2]
    hidden = all_ref.shape[2]
    value = all_ref[0].astype(F32)
    for k in range(shards):
        at = pl.multiple_of((at_ref[0] ^ k) * hidden, hidden)
        up_ref[:, pl.ds(at, hidden)] = value[k * step_rows:(k + 1) * step_rows]
    down_ref[...] = value[shards * step_rows:]


def place_ff(at, gathered, shards, step_rows):
    owners, rows, width = gathered.shape
    down_rows = rows - shards * step_rows
    return pl.pallas_call(
        ff_place_kernel,
        grid_spec=pltpu.PrefetchScalarGridSpec(
            num_scalar_prefetch=1,
            grid=(owners,),
            in_specs=[pl.BlockSpec((1, rows, width), lambda i, at: (i, 0, 0))],
        out_specs=[pl.BlockSpec((step_rows, shards * width), lambda i, core: (i, 0)),
                       pl.BlockSpec((down_rows, width), lambda i, core: (i, 0))],
        ),
        out_shape=[jax.ShapeDtypeStruct((owners * step_rows, shards * width), F32),
                   jax.ShapeDtypeStruct((owners * down_rows, width), F32)],
        compiler_params=pltpu.CompilerParams(vmem_limit_bytes=VMEM_LIMIT),
        name="place_ff",
    )(at, gathered)


def io_place_kernel(cols, core_ref, mine_ref, other_ref, in_ref, out_ref, line_ref):
    parity = pl.program_id(0)
    own = parity == core_ref[0]
    count, rows, width = mine_ref.shape
    half = rows // 2
    groups = width // cols
    held = count // groups
    for g in range(groups):
        value = None
        for i in range(held):
            at = g * held + i
            one = jnp.where(own, mine_ref[at].astype(F32), other_ref[at].astype(F32))
            value = one if value is None else value + one
        for part in range(3):
            at = part * width + g * cols
            in_ref[:, at:at + cols] = value[half:, part * cols:(part + 1) * cols]
        if g == 0:
            out_ref[...] = value[:half]
            line_ref[...] = value[half:, 3 * cols:]
        else:
            out_ref[...] += value[:half]
            line_ref[...] += value[half:, 3 * cols:]


def place_io(core, mine, other, cols):
    count, rows, width = mine.shape
    half = rows // 2
    return pl.pallas_call(
        functools.partial(io_place_kernel, cols),
        grid_spec=pltpu.PrefetchScalarGridSpec(
            num_scalar_prefetch=1,
            grid=(2,),
            in_specs=[whole(mine.shape), whole(other.shape)],
            out_specs=[pl.BlockSpec((half, 3 * width), lambda i, core: (i, 0)),
                       pl.BlockSpec((half, width), lambda i, core: (i, 0)),
                       pl.BlockSpec((half, width - 3 * cols), lambda i, core: (i, 0))],
        ),
        out_shape=[jax.ShapeDtypeStruct((rows, 3 * width), F32), jax.ShapeDtypeStruct((rows, width), F32),
                   jax.ShapeDtypeStruct((rows, width - 3 * cols), F32)],
        compiler_params=pltpu.CompilerParams(vmem_limit_bytes=VMEM_LIMIT),
        name="place_io",
    )(core[None], mine, other)


def spread_out(pieces, axis, groups=None):
    return lax.all_to_all(pieces, axis, 0, 0, axis_index_groups=groups)


def to_all_value(x, count):
    return jnp.broadcast_to(x[None], (count,) + x.shape)


def to_all(x, axis, groups=None, count=None):
    return spread_out(to_all_value(x, count or lax.axis_size(axis)), axis, groups)


def at_distance(pieces):
    count = len(pieces)
    return [pieces[0]] + [
        lax.ppermute(pieces[k], "fsdp", [(i, i ^ k) for i in range(count)]) for k in range(1, count)]


def by_distance(pieces, shard):
    return at_distance([
        lax.dynamic_index_in_dim(pieces, shard ^ k, 0, keepdims=False) for k in range(pieces.shape[0])])


def total(values):
    result = values[0].astype(F32)
    for v in values[1:]:
        result = result + v.astype(F32)
    return result


def after(index, value):
    first = value[(0,) * value.ndim]
    return index + (first != first).astype(jnp.int32)


def on_device(
    inputs, positions, in_weight, in_bias, out_weight, out_bias, up_weight, up_bias, down_weight, down_bias,
    first_gain, first_shift, second_gain, second_shift, out_grad,
):
    x, grad, place = inputs[0], out_grad[0], positions[0]
    tokens, width = x.shape
    owners, shards = lax.axis_size("ctx"), lax.axis_size("fsdp")
    here, shard = lax.axis_index("ctx"), lax.axis_index("fsdp")
    heads = width // HEAD
    groups = math.gcd(heads, owners // 2)
    sharers = owners // groups
    own_heads = heads // groups
    cols = own_heads * HEAD
    group, sharer, core = here // sharers, here % sharers, here % 2
    hidden = down_weight.shape[0]
    rows = in_weight.shape[0]
    half = rows // 2
    length = tokens * owners
    held = tokens // RUN
    joined = hidden == width
    tiles = length // TILE
    parity = [[i for i in range(owners) if i % 2 == k] for k in (0, 1)]
    pairs = [(i, i ^ 1) for i in range(owners)]

    def swap(value):
        return lax.ppermute(value, "ctx", pairs)

    def both(mine, other):
        return jnp.stack([jnp.where(core == 0, mine, other), jnp.where(core == 0, other, mine)], 1)

    run_rows = jnp.broadcast_to(jnp.pad((place[::RUN] // RUN).astype(BF), (0, width - held))[None], (16, width))
    both_all = lax.all_gather(jnp.concatenate([x, grad, run_rows], 0), "ctx", axis=0, tiled=False)

    def block(values):
        lines = [jnp.pad(v[None], ((0, 0), (0, width - v.shape[0]))) for v in values]
        return jnp.pad(jnp.concatenate(lines, 0), ((0, 16 - len(values)), (0, 0)))

    small_block = block([second_gain, second_shift])
    smalls = [in_bias, out_bias, down_bias, first_gain, first_shift]

    def own_half(value, at=core):
        return lax.dynamic_slice_in_dim(value, at * half, half, 0)

    up_pieces = own_half(up_weight).reshape(half, shards, hidden).transpose(1, 0, 2)
    shared = to_all_value(jnp.concatenate([x, grad, small_block], 0), shards)
    skip = -(-(2 * tokens + 16) // (half // 2)) * (half // 2)
    if joined:
        gap = jnp.zeros((shards, skip - 2 * tokens - 16, width), BF)
        plane = spread_out(jnp.concatenate([shared, gap, up_pieces], 1), "fsdp")
        up_own = plane[:, skip:]
    else:
        plane, up_own = spread_out(shared, "fsdp"), spread_out(up_pieces, "fsdp")
    later = after(core, plane)
    in_own = own_half(in_weight, later).reshape(half, 3, groups, cols)
    in_own = lax.dynamic_index_in_dim(in_own, group, 2, keepdims=False).reshape(half, 3 * cols)
    in_own = jnp.pad(in_own, ((0, 0), (0, width - 3 * cols)))
    io_send = to_all_value(jnp.concatenate([own_half(out_weight, later), in_own, block(smalls)], 0), shards)
    io_got = spread_out(io_send, "fsdp")
    small_got, io_got = io_got[:, 2 * half:].astype(F32), io_got[:, :2 * half]

    full_in_bias, full_out_bias, full_down_bias, gain_one, shift_one = [
        small_got[:, i, :s.shape[0]].reshape(-1) for i, s in enumerate(smalls)]

    small_step = rows // owners
    packed = joined and small_step % 8 == 0
    up_other, up_bias_row = swap(up_own), up_bias.astype(F32)[None]
    *ff_parts, up_part, down_part, up_bias_part, gain_two_part, shift_two_part = feed_forward(
        jnp.stack([core, shard]), plane, tokens, plane if joined else up_own, up_other, skip, down_weight,
        up_bias_row, owners if packed else 0)

    def give_half(pieces, axis, mine=core):
        keep = lax.dynamic_index_in_dim(pieces, mine, axis, keepdims=False)
        give = lax.dynamic_index_in_dim(pieces, 1 - mine, axis, keepdims=False)
        return (keep.astype(F32) + swap(give).astype(F32)).astype(BF)

    def reduce_owners(pieces):
        return lax.psum_scatter(pieces, "ctx", scatter_dimension=0, tiled=False)

    def gather_owners(value, earlier):
        mine = to_all(value, "ctx", parity, owners // 2) + after(jnp.int32(0), earlier).astype(BF)
        return mine, swap(mine)

    cut = shards * small_step
    if packed:
        summed = reduce_owners(up_part + after(jnp.int32(0), both_all).astype(BF))
        up_sum, down_sum = summed[:cut], summed[cut:]
    else:
        up_pieces = up_part.reshape(shards, owners, small_step, hidden).transpose(1, 0, 2, 3)
        up_sum = reduce_owners(up_pieces.reshape(owners, cut, hidden))
        down_sum = reduce_owners(down_part.reshape(owners, hidden // owners, width))

    io_got = io_got + after(jnp.int32(0), ff_parts[0]).astype(BF)
    io_full = both(io_got, swap(io_got)).reshape(shards, 2, 2, half, width)
    out_full = io_full[:, :, 0].reshape(width, width)
    in_full = io_full[:, :, 1].reshape(width, width)[:, :3 * cols].T
    out_own = lax.dynamic_slice_in_dim(out_full, group * cols, cols, 0)
    run_at = both_all[:, 2 * tokens, :held].reshape(-1).astype(jnp.int32)
    runs = run_at.shape[0]
    at_run = lax.broadcasted_iota(jnp.int32, (runs, runs), 0)
    of_run = lax.broadcasted_iota(jnp.int32, (runs, runs), 1)
    order = jnp.sum(jnp.where(run_at[None] == at_run, of_run, 0), 1)

    ladder = 10000.0 ** (-jnp.arange(0, ROT, 2, dtype=F32) / ROT)
    angle = jnp.arange(length, dtype=jnp.int32).astype(F32).reshape(tiles, 1, TILE) * ladder[None, :, None]
    cosine, sine = jnp.cos(angle), jnp.sin(angle)

    bias_own = lax.dynamic_index_in_dim(full_in_bias.reshape(3, groups, cols), group, 1, keepdims=False)
    qkv = project(order, both_all, in_full, out_own, bias_own.reshape(-1, 1), gain_one[None], shift_one[None],
                  cosine, sine)
    spots = jnp.concatenate([sharer[None].astype(jnp.int32), order])
    ff_got = at_distance(ff_parts)
    mixed_out, back_qkv = attend(spots, qkv, cosine, sine, owners, sharers)
    up_sum = jnp.concatenate(by_distance(up_sum.reshape(shards, small_step, hidden), after(shard, back_qkv)), 0)
    mixed_own = give_half(mixed_out.reshape(owners // 2, 2, own_heads, held, HEAD, RUN), 1)
    mixed_got = spread_out(mixed_own, "ctx", parity)
    if joined:
        ff_own = jnp.concatenate([up_sum, down_sum], 0)
        ff_all = lax.all_gather(ff_own, "ctx", axis=0, tiled=False)
        up_all, down_all = ff_all[:, :cut], ff_all[:, cut:]
    else:
        ff_own = up_sum
        up_all, down_all = [lax.all_gather(v, "ctx", axis=0, tiled=False) for v in (up_sum, down_sum)]
    x32, grad32 = x.astype(F32), grad.astype(F32)
    gain_row, shift_row = gain_one[None], shift_one[None]
    in_part, out_part, in_bias_part, gain_one_part, shift_one_part = back_to_weight(
        order, back_qkv, in_full, both_all, mixed_out, gain_row, shift_row, (mixed_own, ff_own))
    if packed:
        up_weight_gradient, down_weight_gradient = place_ff(shard[None], ff_all, shards, small_step)
    else:
        up_all = up_all.reshape(owners, shards, small_step, hidden)
        up_all = [lax.dynamic_index_in_dim(up_all, shard ^ f, 1, keepdims=False) for f in range(shards)]
        up_weight_gradient = jnp.concatenate(up_all, -1).reshape(rows, shards * hidden).astype(F32)
        down_weight_gradient = down_all.reshape(hidden, width).astype(F32)

    mixed_got = mixed_got + after(jnp.int32(0), in_part).astype(BF)
    ff_sum = total(ff_got) + after(jnp.int32(0), down_weight_gradient).astype(F32)
    mixed = jnp.sum(mixed_got.astype(F32).reshape(groups, sharers // 2, own_heads, held, HEAD, RUN), 1)
    mixed = mixed.transpose(0, 1, 3, 2, 4).reshape(width, tokens).astype(BF)
    branch = mm(mixed, out_full, (0, 0))
    output = x32 + (branch + full_out_bias) + (ff_sum[:tokens] + full_down_bias)

    in_bias_full = lax.dynamic_update_slice_in_dim(
        jnp.zeros((3, groups, cols), F32), in_bias_part.reshape(3, 1, cols), group, 1)
    lines = [in_bias_full.reshape(-1), jnp.sum(grad32, 0), gain_one_part[0], shift_one_part[0], gain_two_part[0],
             shift_two_part[0]]
    lines = [v.reshape(shards, -1) for v in lines]
    at_shard = (jnp.arange(shards) == shard)[:, None]
    lines.append(jnp.where(at_shard, up_bias_part, 0.0))
    line_sizes = [v.shape[1] for v in lines]
    lines = jnp.concatenate(lines, 1).astype(BF).reshape(shards, 2, -1, width - 3 * cols)
    line_rows = lines.shape[2]
    lines = jnp.pad(lines, ((0, 0), (0, 0), (0, half - line_rows), (0, 0)))
    out_rows = lax.dynamic_update_slice_in_dim(
        jnp.zeros((width, width), BF), out_part.astype(BF), group * cols, 0)
    in_pieces = jnp.concatenate([in_part.reshape(shards, 2, half, 3 * cols), lines], 3)
    pieces = jnp.concatenate([out_rows.reshape(shards, 2, half, width), in_pieces], 2)
    pieces = give_half(pieces, 1, after(core, mixed_got))
    e_runs = back_to_input(order, back_qkv, in_full, gain_row, (pieces, pieces))
    e_sum = lax.psum_scatter(e_runs.reshape(length, width), "ctx", scatter_dimension=0, tiled=True)
    pieces = total(by_distance(pieces, shard)).astype(BF)
    pieces = pieces + after(jnp.int32(0), down_weight_gradient).astype(BF)
    in_weight_gradient, out_weight_gradient, line_sum = place_io(
        core, *gather_owners(pieces, output), cols)
    line_sum = line_sum.reshape(2, half, -1)[:, :line_rows].reshape(-1)
    totals, at = [], 0
    for size in line_sizes:
        totals.append(line_sum[at:at + size])
        at += size

    e = e_sum.astype(F32) + ff_sum[tokens:]
    xhat, inverse = normalize(x32)
    input_gradient = grad32 + inverse * (
        e - jnp.mean(e, -1, keepdims=True) - xhat * jnp.mean(e * xhat, -1, keepdims=True))
    return (
        output.astype(BF)[None], input_gradient[None], in_weight_gradient, totals[0], out_weight_gradient, totals[1],
        up_weight_gradient, totals[6], down_weight_gradient, totals[1], totals[2], totals[3], totals[4], totals[5],
    )


def solution(mesh):
    token, matrix, vector = P("fsdp", "ctx", None), P("fsdp", None), P("fsdp")
    return jax.shard_map(
        on_device,
        mesh=mesh,
        in_specs=(token, P("fsdp", "ctx"), matrix, vector, matrix, vector, matrix, vector, matrix, vector,
                  vector, vector, vector, vector, token),
        out_specs=(token, token, matrix, vector, matrix, vector, matrix, vector, matrix, vector,
                   vector, vector, vector, vector),
        check_vma=False,
    )
```

```python
import functools
import math

import jax
import jax.numpy as jnp
from jax import lax
from jax.experimental import pallas as pl
from jax.experimental.pallas import tpu as pltpu
from jax.sharding import PartitionSpec as P

HEAD = 64
ROT = 16
HALF = ROT // 2
RUN = 128
TILE = 256
SUB = 256
NEG = -1e30
EPS = 1e-05
BF = jnp.bfloat16
F32 = jnp.float32
VMEM_LIMIT = 60 * 1024 * 1024


def mm(left, right, dims):
    return lax.dot_general(left, right, ((dims[:1], dims[1:]), ((), ())), preferred_element_type=F32)


def flip(x):
    return x.astype(F32).T.astype(x.dtype)


def normalize(values):
    mean = jnp.mean(values, -1, keepdims=True)
    centred = values - mean
    spread = jnp.mean(centred * centred, -1, keepdims=True)
    inverse = lax.rsqrt(spread + EPS)
    return centred * inverse, inverse


def turn(values, cosine, sine):
    one, two = values[:HALF], values[HALF:ROT]
    return jnp.concatenate([one * cosine - two * sine, two * cosine + one * sine, values[ROT:]], 0)


def ff_kernel(packed, core_ref, x_ref, g_ref, small_ref, mine_ref, mine_end_ref, other_ref, down_ref, upb_ref,
              *refs):
    shards = small_ref.shape[0]
    outs, refs = refs[:shards], refs[shards:]
    (dup_ref, ddown_ref, dbias_ref, dgain_ref, dshift_ref, acc_up, acc_down, up_ref, gain_ref, shift_ref) = refs
    step = pl.program_id(0)

    @pl.when(step == 0)
    def _():
        half = other_ref.shape[1]
        share = gain_ref.shape[1] // shards
        first = core_ref[0] == 0
        for f in range(shards):
            mine = jnp.concatenate([mine_ref[f].astype(F32), mine_end_ref[f].astype(F32)], 0)
            other = other_ref[f].astype(F32)
            at = 2 * f * half
            up_ref[at:at + half] = jnp.where(first, mine, other).astype(BF)
            up_ref[at + half:at + 2 * half] = jnp.where(first, other, mine).astype(BF)
            small = small_ref[f].astype(F32)
            gain_ref[:, f * share:(f + 1) * share] = small[0:1, :share]
            shift_ref[:, f * share:(f + 1) * share] = small[1:2, :share]
        acc_up[...] = jnp.zeros_like(acc_up)
        acc_down[...] = jnp.zeros_like(acc_down)
        dbias_ref[...] = jnp.zeros_like(dbias_ref)
        dgain_ref[...] = jnp.zeros_like(dgain_ref)
        dshift_ref[...] = jnp.zeros_like(dshift_ref)

    grad = g_ref[0]
    back_active = mm(grad, down_ref[...], (1, 1))
    xhat, _ = normalize(x_ref[0].astype(F32))
    second = (xhat * gain_ref[...] + shift_ref[...]).astype(BF)
    up = mm(second, up_ref[...], (1, 0)) + upb_ref[...]
    phi = 0.5 * (1.0 + lax.erf(up * (1.0 / math.sqrt(2.0))))
    active = (up * phi).astype(BF)
    slope = phi + up * jnp.exp(-0.5 * up * up) * (1.0 / math.sqrt(2.0 * math.pi))
    tokens = x_ref.shape[1]
    part = mm(active, down_ref[...], (1, 0)).astype(BF)
    low_up = (back_active * slope).astype(BF)
    dbias_ref[...] += jnp.sum(low_up.astype(F32), 0, keepdims=True)
    acc_up[...] += mm(second, low_up, (0, 0))
    acc_down[...] += mm(active, grad, (0, 0))
    back = mm(low_up, up_ref[...], (1, 1))
    dgain_ref[...] += jnp.sum(back * xhat, 0, keepdims=True)
    dshift_ref[...] += jnp.sum(back, 0, keepdims=True)
    back = (back * gain_ref[...]).astype(BF)
    for k in range(shards):
        @pl.when(step == k)
        def _(k=k):
            outs[k][:tokens] = part
            outs[k][tokens:] = back

    @pl.when(step == pl.num_programs(0) - 1)
    def _():
        if packed:
            owners = dup_ref.shape[0]
            rows = acc_up.shape[0] // shards
            few = rows // owners
            down_rows = acc_down.shape[0] // owners
            for c in range(owners):
                up_rows = [acc_up[f * rows + c * few:f * rows + (c + 1) * few] for f in range(shards)]
                dup_ref[c] = jnp.concatenate(
                    up_rows + [acc_down[c * down_rows:(c + 1) * down_rows]], 0).astype(BF)
            ddown_ref[...] = jnp.zeros_like(ddown_ref)
        else:
            dup_ref[...] = acc_up[...].astype(BF)
            ddown_ref[...] = acc_down[...].astype(BF)


ANY = pl.BlockSpec(memory_space=pl.ANY)


def whole(shape):
    return pl.BlockSpec(shape, lambda *_: (0,) * len(shape))


def cost(macs, size):
    return pl.CostEstimate(flops=int(2 * macs), bytes_accessed=int(size), transcendentals=0)


def feed_forward(at, got, tokens, up_mine, up_other, skip, down, up_bias, owners):
    groups, _, width = got.shape
    hidden = down.shape[0]
    half = width // groups // 2
    quarter = half // 2
    at_up = skip // quarter if up_mine is got else 0
    x_tile = pl.BlockSpec((1, tokens, width), lambda i, at: (at[1] ^ i, 0, 0))
    g_tile = pl.BlockSpec((1, tokens, width), lambda i, at: (at[1] ^ i, 1, 0))
    small_tile = pl.BlockSpec((groups, 16, width), lambda i, at: (0, 2 * tokens // 16, 0))
    row = jax.ShapeDtypeStruct((1, width), F32)
    if owners:
        shapes = [(owners, (width + hidden) // owners, hidden), (16, 128)]
    else:
        shapes = [(width, hidden), (hidden, width)]
    return pl.pallas_call(
        functools.partial(ff_kernel, bool(owners)),
        grid_spec=pltpu.PrefetchScalarGridSpec(
            num_scalar_prefetch=1,
            grid=(groups,),
            in_specs=[x_tile, g_tile, small_tile,
                      pl.BlockSpec((groups, quarter, hidden), lambda i, at: (0, at_up, 0)),
                      pl.BlockSpec((groups, quarter, hidden), lambda i, at: (0, at_up + 1, 0)),
                      whole((groups, half, hidden)), whole((hidden, width)), whole((1, hidden))],
            out_specs=[whole((2 * tokens, width))] * groups + [whole(shape) for shape in shapes]
            + [whole((1, hidden)), whole((1, width)), whole((1, width))],
            scratch_shapes=[pltpu.VMEM((width, hidden), F32), pltpu.VMEM((hidden, width), F32),
                            pltpu.VMEM((width, hidden), BF), pltpu.VMEM((1, width), F32),
                            pltpu.VMEM((1, width), F32)],
        ),
        out_shape=[jax.ShapeDtypeStruct((2 * tokens, width), BF)] * groups
        + [jax.ShapeDtypeStruct(shape, BF) for shape in shapes]
        + [jax.ShapeDtypeStruct((1, hidden), F32), row, row],
        compiler_params=pltpu.CompilerParams(vmem_limit_bytes=VMEM_LIMIT),
        cost_estimate=cost(12 * groups * tokens * width * hidden, 4 * got.size),
        name="feed_forward",
    )(at, got, got, got, up_mine, up_mine, up_other, down, up_bias)


def qkv_kernel(order_ref, xa_ref, xb_ref, ga_ref, gb_ref, w_ref, wo_ref, bias_ref, gain_ref, shift_ref, cos_ref,
               sin_ref, out_ref):
    back = mm(wo_ref[...], jnp.concatenate([ga_ref[0], gb_ref[0]], 0), (1, 1)).astype(BF)
    values = jnp.concatenate([xa_ref[0], xb_ref[0]], 0).astype(F32)
    xhat, _ = normalize(values)
    first = (xhat * gain_ref[...] + shift_ref[...]).astype(BF)
    proj = mm(w_ref[...], first, (1, 1)) + bias_ref[...]
    heads = out_ref.shape[0] // 4
    cosine, sine = cos_ref[0], sin_ref[0]
    for i in range(3 * heads):
        part = proj[i * HEAD:(i + 1) * HEAD]
        if i < 2 * heads:
            part = turn(part, cosine, sine)
        part = part.astype(BF)
        if i < heads:
            part = part * jnp.asarray(1.0 / math.sqrt(HEAD), BF)
        out_ref[i, 0] = part
    for i in range(heads):
        out_ref[3 * heads + i, 0] = back[i * HEAD:(i + 1) * HEAD]


def run_specs(width, held, skip):
    def at(i, order, k):
        run = order[2 * i + k]
        return run // held, run % held + skip, 0

    return [pl.BlockSpec((1, RUN, width), lambda i, order, k=k: at(i, order, k)) for k in (0, 1)]


def project(order, both_all, w, w_out, bias, gain, shift, cosine, sine):
    owners, _, width = both_all.shape
    held = order.shape[0] // owners
    rows, cols = w.shape[0], w_out.shape[0]
    tiles = order.shape[0] // 2
    parts = (rows + cols) // HEAD
    table = pl.BlockSpec((1, HALF, TILE), lambda i, order: (i, 0, 0))
    return pl.pallas_call(
        qkv_kernel,
        grid_spec=pltpu.PrefetchScalarGridSpec(
            num_scalar_prefetch=1,
            grid=(tiles,),
            in_specs=run_specs(width, held, 0) + run_specs(width, held, held)
            + [whole((rows, width)), whole((cols, width)), whole((rows, 1)), whole((1, width)),
               whole((1, width)), table, table],
            out_specs=pl.BlockSpec((parts, 1, HEAD, TILE), lambda i, order: (0, i, 0, 0)),
        ),
        out_shape=jax.ShapeDtypeStruct((parts, tiles, HEAD, TILE), BF),
        compiler_params=pltpu.CompilerParams(vmem_limit_bytes=VMEM_LIMIT),
        cost_estimate=cost(5 * tiles * TILE * width * (rows + cols), 4 * both_all.size),
        name="project",
    )(order, both_all, both_all, both_all, both_all, w, w_out, bias, gain, shift, cosine, sine)


def attention_kernel(share, fused, held, place_ref, q_ref, k_ref, v_ref, d_ref, cos_ref, sin_ref,
                     mix_ref, back_ref, keys, values, dkeys, dvalues, sbuf, pbuf):
    turn_at, step = pl.program_id(0), pl.program_id(1)
    heads, steps = pl.num_programs(0) * fused, pl.num_programs(1)
    tiles = k_ref.shape[1]
    block = share(step, place_ref)
    every = range(fused)

    @pl.when((turn_at == 0) & (step == 0))
    def _():
        mix_ref[...] = jnp.zeros_like(mix_ref)
        queries_end = back_ref.shape[0] // 3
        back_ref[:queries_end] = jnp.zeros((queries_end,) + back_ref.shape[1:], BF)

    @pl.when(step == 0)
    def _():
        @pl.loop(0, tiles)
        def _(j):
            for h in every:
                keys[h, j] = flip(k_ref[h, j])
                values[h, j] = flip(v_ref[h, j])
                dkeys[h, j] = jnp.zeros((TILE, HEAD), F32)
                dvalues[h, j] = jnp.zeros((TILE, HEAD), F32)

    queries = [q_ref[h, 0] for h in every]

    def fold(x, op):
        return op(x.reshape(x.shape[0] // 8, 8, TILE), 0)

    pieces = [(h, slice(i, i + SUB)) for h in every for i in range(0, TILE, SUB)]

    def score(j, peaks):
        new = list(peaks)
        for h, at in pieces:
            s = mm(keys[h, j, at], queries[h], (1, 0))
            sbuf[h, j, at] = s
            new[h] = jnp.maximum(new[h], fold(s, jnp.max))
        return tuple(new)

    peaks = lax.fori_loop(0, block, score, tuple(jnp.full((8, TILE), NEG, F32) for _ in every))
    key_at = lax.broadcasted_iota(jnp.int32, (TILE, TILE), 0)
    query_at = lax.broadcasted_iota(jnp.int32, (TILE, TILE), 1)
    last = []
    for h in every:
        s = jnp.where(key_at <= query_at, mm(keys[h, block], queries[h], (1, 0)), NEG)
        sbuf[h, block] = s
        last.append(jnp.max(jnp.maximum(peaks[h], fold(s, jnp.max)), 0, keepdims=True))
    peaks = last

    def weigh(j, carry):
        new = list(carry)
        for h, at in pieces:
            total, mixed = new[h]
            p = jnp.exp(sbuf[h, j, at] - peaks[h])
            low = p.astype(BF)
            pbuf[h, j, at] = low
            new[h] = (total + fold(p, jnp.sum), mixed)
        for h, at in pieces:
            total, mixed = new[h]
            new[h] = (total, mixed + mm(v_ref[h, j, :, at], pbuf[h, j, at], (1, 0)))
        return tuple(new)

    sums = lax.fori_loop(
        0, block + 1, weigh,
        tuple((jnp.zeros((8, TILE), F32), jnp.zeros((HEAD, TILE), F32)) for _ in every))
    spreads, backs, back_rows, query_rows = [], [], [], []
    for h in every:
        total, mixed = sums[h]
        inverse = 1.0 / jnp.sum(total, 0, keepdims=True)
        mixed = mixed * inverse
        low_mixed = mixed.astype(BF)
        for k in (0, 1):
            at = place_ref[1 + 2 * block + k]
            mix_ref[at // held, turn_at * fused + h, at % held] = low_mixed[:, k * RUN:(k + 1) * RUN]
        back = d_ref[h, 0].astype(F32) * inverse
        spreads.append(jnp.sum(back * mixed, 0, keepdims=True))
        back = back.astype(BF)
        backs.append(back)
        back_rows.append(flip(back))
        query_rows.append(flip(queries[h]))

    def pull(j, dquery):
        new = list(dquery)

        def finish(h, at, dp):
            low = pbuf[h, j, at]
            ds = (low.astype(F32) * (dp - spreads[h])).astype(BF)
            dvalues[h, j, at] += mm(low, back_rows[h], (1, 0))
            dkeys[h, j, at] += mm(ds, query_rows[h], (1, 0))
            new[h] = new[h] + mm(k_ref[h, j, :, at], ds, (1, 0))

        dps = [mm(values[h, j, at], backs[h], (1, 0)) for h, at in pieces]
        for (h, at), dp in zip(pieces, dps):
            finish(h, at, dp)
        return tuple(new)

    dquery = lax.fori_loop(0, block + 1, pull, tuple(jnp.zeros((HEAD, TILE), F32) for _ in every))
    for h in every:
        dq = dquery[h] * (1.0 / math.sqrt(HEAD))
        back_ref[turn_at * fused + h, block] = turn(dq, cos_ref[block], -sin_ref[block]).astype(BF)

    @pl.when(step == steps - 1)
    def _():
        @pl.loop(0, tiles)
        def _(j):
            for h in every:
                at = heads + turn_at * fused + h
                back_ref[at, j] = turn(dkeys[h, j].T, cos_ref[j], -sin_ref[j]).astype(BF)
                back_ref[heads + at, j] = dvalues[h, j].T.astype(BF)


def attend(place, qkv, cosine, sine, owners, sharers):
    parts, tiles, _, _ = qkv.shape
    heads = parts // 4
    held = (place.shape[0] - 1) // owners
    steps = tiles // sharers
    fused = heads if tiles <= 16 else 1
    turns = heads // fused

    def share(step, place_ref):
        return 2 * sharers * (step // 2) + jnp.where(step % 2 == 0, place_ref[0], 2 * sharers - 1 - place_ref[0])

    all_tiles, one_tile = (fused, tiles, HEAD, TILE), (fused, 1, HEAD, TILE)
    return pl.pallas_call(
        functools.partial(attention_kernel, share, fused, held),
        grid_spec=pltpu.PrefetchScalarGridSpec(
            num_scalar_prefetch=1,
            grid=(turns, steps),
            in_specs=[
                pl.BlockSpec(one_tile, lambda h, n, p: (h, share(n, p), 0, 0)),
                pl.BlockSpec(all_tiles, lambda h, n, p: (turns + h, 0, 0, 0)),
                pl.BlockSpec(all_tiles, lambda h, n, p: (2 * turns + h, 0, 0, 0)),
                pl.BlockSpec(one_tile, lambda h, n, p: (3 * turns + h, share(n, p), 0, 0)),
                whole((tiles, HALF, TILE)),
                whole((tiles, HALF, TILE)),
            ],
            out_specs=[whole((owners, heads, held, HEAD, RUN)), whole((3 * heads, tiles, HEAD, TILE))],
            scratch_shapes=[
                pltpu.VMEM((fused, tiles, TILE, HEAD), BF),
                pltpu.VMEM((fused, tiles, TILE, HEAD), BF),
                pltpu.VMEM((fused, tiles, TILE, HEAD), F32),
                pltpu.VMEM((fused, tiles, TILE, HEAD), F32),
                pltpu.VMEM((fused, tiles, TILE, TILE), F32),
                pltpu.VMEM((fused, tiles, TILE, TILE), BF),
            ],
        ),
        out_shape=[jax.ShapeDtypeStruct((owners, heads, held, HEAD, RUN), BF),
                   jax.ShapeDtypeStruct((3 * heads, tiles, HEAD, TILE), BF)],
        compiler_params=pltpu.CompilerParams(vmem_limit_bytes=VMEM_LIMIT),
        cost_estimate=cost(40 * heads * HEAD * tiles * TILE * steps * TILE, 4 * qkv.size),
        name="attend",
    )(place, qkv, qkv, qkv, qkv, cosine, sine)


def back_weight_kernel(order_ref, b_ref, w_ref, xa_ref, xb_ref, ga_ref, gb_ref, ma_ref, mb_ref, gain_ref, shift_ref,
                       _, __, dw_ref, dout_ref, dbias_ref, dgain_ref, dshift_ref, acc):
    step = pl.program_id(0)

    @pl.when(step == 0)
    def _():
        acc[...] = jnp.zeros_like(acc)
        dout_ref[...] = jnp.zeros_like(dout_ref)
        dbias_ref[...] = jnp.zeros_like(dbias_ref)

    rows, cols = b_ref.shape[0] * HEAD, ma_ref.shape[1] * HEAD
    mixed = jnp.concatenate([r[0, :, 0].reshape(cols, RUN) for r in (ma_ref, mb_ref)], 1)
    dout_ref[...] += mm(mixed, jnp.concatenate([ga_ref[0], gb_ref[0]], 0), (1, 0))
    xhat, _ = normalize(jnp.concatenate([xa_ref[0], xb_ref[0]], 0).astype(F32))
    back = b_ref[...].reshape(rows, TILE)
    acc[...] += mm(back, xhat.astype(BF), (1, 0))
    dbias_ref[...] += jnp.sum(back.astype(F32), 1, keepdims=True)

    @pl.when(step == pl.num_programs(0) - 1)
    def _():
        weight = w_ref[...].astype(F32)
        bias = dbias_ref[...]
        dgain_ref[...] = jnp.sum(acc[...] * weight, 0, keepdims=True)
        dshift_ref[...] = jnp.sum(bias * weight, 0, keepdims=True)
        dw_ref[...] = (acc[...] * gain_ref[...] + bias * shift_ref[...]).T.astype(BF)


def back_input_kernel(order_ref, b_ref, w_ref, gain_ref, _, __, e_ref):
    step = pl.program_id(0)
    back = b_ref[...].reshape(b_ref.shape[0] * HEAD, TILE)
    e = (mm(back, w_ref[...], (0, 0)) * gain_ref[...]).astype(BF)
    e_ref[order_ref[2 * step]] = e[:RUN]
    e_ref[order_ref[2 * step + 1]] = e[RUN:]


def back_to_weight(order, back, w, both_all, mixed, gain, shift, earlier):
    owners, _, width = both_all.shape
    held = order.shape[0] // owners
    rows = w.shape[0]
    parts, tiles, _, _ = back.shape
    heads = parts // 3
    line = jax.ShapeDtypeStruct((1, width), F32)

    def mixed_at(i, order, k):
        run = order[2 * i + k]
        return run // held, 0, run % held, 0, 0

    mixed_specs = [pl.BlockSpec((1, heads, 1, HEAD, RUN), lambda i, order, k=k: mixed_at(i, order, k)) for k in (0, 1)]
    return pl.pallas_call(
        back_weight_kernel,
        grid_spec=pltpu.PrefetchScalarGridSpec(
            num_scalar_prefetch=1,
            grid=(tiles,),
            in_specs=[pl.BlockSpec((parts, 1, HEAD, TILE), lambda i, order: (0, i, 0, 0)), whole((rows, width))]
            + run_specs(width, held, 0) + run_specs(width, held, held) + mixed_specs
            + [whole((1, width)), whole((1, width)), ANY, ANY],
            out_specs=[whole((width, rows)), whole((heads * HEAD, width)), whole((rows, 1)), whole((1, width)),
                       whole((1, width))],
            scratch_shapes=[pltpu.VMEM((rows, width), F32)],
        ),
        out_shape=[jax.ShapeDtypeStruct((width, rows), BF), jax.ShapeDtypeStruct((heads * HEAD, width), F32),
                   jax.ShapeDtypeStruct((rows, 1), F32), line, line],
        compiler_params=pltpu.CompilerParams(vmem_limit_bytes=VMEM_LIMIT),
        cost_estimate=cost(5 * tiles * TILE * width * rows, 4 * both_all.size),
        name="back_to_weight",
    )(order, back, w, both_all, both_all, both_all, both_all, mixed, mixed, gain, shift, *earlier)


def back_to_input(order, back, w, gain, earlier):
    rows, width = w.shape
    parts, tiles, _, _ = back.shape
    runs = order.shape[0]
    return pl.pallas_call(
        back_input_kernel,
        grid_spec=pltpu.PrefetchScalarGridSpec(
            num_scalar_prefetch=1,
            grid=(tiles,),
            in_specs=[pl.BlockSpec((parts, 1, HEAD, TILE), lambda i, order: (0, i, 0, 0)), whole((rows, width)),
                      whole((1, width)), ANY, ANY],
            out_specs=whole((runs, RUN, width)),
        ),
        out_shape=jax.ShapeDtypeStruct((runs, RUN, width), BF),
        compiler_params=pltpu.CompilerParams(vmem_limit_bytes=VMEM_LIMIT),
        cost_estimate=cost(5 * tiles * TILE * width * rows, 8 * back.size),
        name="back_to_input",
    )(order, back, w, gain, *earlier)


def ff_place_kernel(at_ref, all_ref, up_ref, down_ref):
    step_rows, shards = up_ref.shape[0], up_ref.shape[1] // all_ref.shape[2]
    hidden = all_ref.shape[2]
    value = all_ref[0].astype(F32)
    for k in range(shards):
        at = pl.multiple_of((at_ref[0] ^ k) * hidden, hidden)
        up_ref[:, pl.ds(at, hidden)] = value[k * step_rows:(k + 1) * step_rows]
    down_ref[...] = value[shards * step_rows:]


def place_ff(at, gathered, shards, step_rows):
    owners, rows, width = gathered.shape
    down_rows = rows - shards * step_rows
    return pl.pallas_call(
        ff_place_kernel,
        grid_spec=pltpu.PrefetchScalarGridSpec(
            num_scalar_prefetch=1,
            grid=(owners,),
            in_specs=[pl.BlockSpec((1, rows, width), lambda i, at: (i, 0, 0))],
        out_specs=[pl.BlockSpec((step_rows, shards * width), lambda i, core: (i, 0)),
                       pl.BlockSpec((down_rows, width), lambda i, core: (i, 0))],
        ),
        out_shape=[jax.ShapeDtypeStruct((owners * step_rows, shards * width), F32),
                   jax.ShapeDtypeStruct((owners * down_rows, width), F32)],
        compiler_params=pltpu.CompilerParams(vmem_limit_bytes=VMEM_LIMIT),
        name="place_ff",
    )(at, gathered)


def io_place_kernel(cols, core_ref, mine_ref, other_ref, in_ref, out_ref, line_ref):
    parity = pl.program_id(0)
    own = parity == core_ref[0]
    count, rows, width = mine_ref.shape
    half = rows // 2
    groups = width // cols
    held = count // groups
    for g in range(groups):
        value = None
        for i in range(held):
            at = g * held + i
            one = jnp.where(own, mine_ref[at].astype(F32), other_ref[at].astype(F32))
            value = one if value is None else value + one
        for part in range(3):
            at = part * width + g * cols
            in_ref[:, at:at + cols] = value[half:, part * cols:(part + 1) * cols]
        if g == 0:
            out_ref[...] = value[:half]
            line_ref[...] = value[half:, 3 * cols:]
        else:
            out_ref[...] += value[:half]
            line_ref[...] += value[half:, 3 * cols:]


def place_io(core, mine, other, cols):
    count, rows, width = mine.shape
    half = rows // 2
    return pl.pallas_call(
        functools.partial(io_place_kernel, cols),
        grid_spec=pltpu.PrefetchScalarGridSpec(
            num_scalar_prefetch=1,
            grid=(2,),
            in_specs=[whole(mine.shape), whole(other.shape)],
            out_specs=[pl.BlockSpec((half, 3 * width), lambda i, core: (i, 0)),
                       pl.BlockSpec((half, width), lambda i, core: (i, 0)),
                       pl.BlockSpec((half, width - 3 * cols), lambda i, core: (i, 0))],
        ),
        out_shape=[jax.ShapeDtypeStruct((rows, 3 * width), F32), jax.ShapeDtypeStruct((rows, width), F32),
                   jax.ShapeDtypeStruct((rows, width - 3 * cols), F32)],
        compiler_params=pltpu.CompilerParams(vmem_limit_bytes=VMEM_LIMIT),
        name="place_io",
    )(core[None], mine, other)


def spread_out(pieces, axis, groups=None):
    return lax.all_to_all(pieces, axis, 0, 0, axis_index_groups=groups)


def to_all_value(x, count):
    return jnp.broadcast_to(x[None], (count,) + x.shape)


def to_all(x, axis, groups=None, count=None):
    return spread_out(to_all_value(x, count or lax.axis_size(axis)), axis, groups)


def at_distance(pieces):
    count = len(pieces)
    return [pieces[0]] + [
        lax.ppermute(pieces[k], "fsdp", [(i, i ^ k) for i in range(count)]) for k in range(1, count)]


def by_distance(pieces, shard):
    return at_distance([
        lax.dynamic_index_in_dim(pieces, shard ^ k, 0, keepdims=False) for k in range(pieces.shape[0])])


def total(values):
    result = values[0].astype(F32)
    for v in values[1:]:
        result = result + v.astype(F32)
    return result


def after(index, value):
    first = value[(0,) * value.ndim]
    return index + (first != first).astype(jnp.int32)


def on_device(
    inputs, positions, in_weight, in_bias, out_weight, out_bias, up_weight, up_bias, down_weight, down_bias,
    first_gain, first_shift, second_gain, second_shift, out_grad,
):
    x, grad, place = inputs[0], out_grad[0], positions[0]
    tokens, width = x.shape
    owners, shards = lax.axis_size("ctx"), lax.axis_size("fsdp")
    here, shard = lax.axis_index("ctx"), lax.axis_index("fsdp")
    heads = width // HEAD
    groups = math.gcd(heads, owners // 2)
    sharers = owners // groups
    own_heads = heads // groups
    cols = own_heads * HEAD
    group, sharer, core = here // sharers, here % sharers, here % 2
    hidden = down_weight.shape[0]
    rows = in_weight.shape[0]
    half = rows // 2
    length = tokens * owners
    held = tokens // RUN
    joined = hidden == width
    tiles = length // TILE
    parity = [[i for i in range(owners) if i % 2 == k] for k in (0, 1)]
    pairs = [(i, i ^ 1) for i in range(owners)]

    def swap(value):
        return lax.ppermute(value, "ctx", pairs)

    def both(mine, other):
        return jnp.stack([jnp.where(core == 0, mine, other), jnp.where(core == 0, other, mine)], 1)

    run_rows = jnp.broadcast_to(jnp.pad((place[::RUN] // RUN).astype(BF), (0, width - held))[None], (16, width))
    both_all = lax.all_gather(jnp.concatenate([x, grad, run_rows], 0), "ctx", axis=0, tiled=False)

    def block(values):
        lines = [jnp.pad(v[None], ((0, 0), (0, width - v.shape[0]))) for v in values]
        return jnp.pad(jnp.concatenate(lines, 0), ((0, 16 - len(values)), (0, 0)))

    small_block = block([second_gain, second_shift])
    smalls = [in_bias, out_bias, down_bias, first_gain, first_shift]

    def own_half(value, at=core):
        return lax.dynamic_slice_in_dim(value, at * half, half, 0)

    up_pieces = own_half(up_weight).reshape(half, shards, hidden).transpose(1, 0, 2)
    shared = to_all_value(jnp.concatenate([x, grad, small_block], 0), shards)
    skip = -(-(2 * tokens + 16) // (half // 2)) * (half // 2)
    if joined:
        gap = jnp.zeros((shards, skip - 2 * tokens - 16, width), BF)
        plane = spread_out(jnp.concatenate([shared, gap, up_pieces], 1), "fsdp")
        up_own = plane[:, skip:]
    else:
        plane, up_own = spread_out(shared, "fsdp"), spread_out(up_pieces, "fsdp")
    later = after(core, plane)
    in_own = own_half(in_weight, later).reshape(half, 3, groups, cols)
    in_own = lax.dynamic_index_in_dim(in_own, group, 2, keepdims=False).reshape(half, 3 * cols)
    in_own = jnp.pad(in_own, ((0, 0), (0, width - 3 * cols)))
    io_send = to_all_value(jnp.concatenate([own_half(out_weight, later), in_own, block(smalls)], 0), shards)
    io_got = spread_out(io_send, "fsdp")
    small_got, io_got = io_got[:, 2 * half:].astype(F32), io_got[:, :2 * half]

    full_in_bias, full_out_bias, full_down_bias, gain_one, shift_one = [
        small_got[:, i, :s.shape[0]].reshape(-1) for i, s in enumerate(smalls)]

    small_step = rows // owners
    packed = joined and small_step % 8 == 0
    up_other, up_bias_row = swap(up_own), up_bias.astype(F32)[None]
    *ff_parts, up_part, down_part, up_bias_part, gain_two_part, shift_two_part = feed_forward(
        jnp.stack([core, shard]), plane, tokens, plane if joined else up_own, up_other, skip, down_weight,
        up_bias_row, owners if packed else 0)

    def give_half(pieces, axis, mine=core):
        keep = lax.dynamic_index_in_dim(pieces, mine, axis, keepdims=False)
        give = lax.dynamic_index_in_dim(pieces, 1 - mine, axis, keepdims=False)
        return (keep.astype(F32) + swap(give).astype(F32)).astype(BF)

    def reduce_owners(pieces):
        return lax.psum_scatter(pieces, "ctx", scatter_dimension=0, tiled=False)

    def gather_owners(value):
        mine = to_all(value, "ctx", parity, owners // 2)
        return mine, swap(mine)

    cut = shards * small_step
    if packed:
        summed = reduce_owners(up_part + after(jnp.int32(0), both_all).astype(BF))
        up_sum, down_sum = summed[:cut], summed[cut:]
    else:
        up_pieces = up_part.reshape(shards, owners, small_step, hidden).transpose(1, 0, 2, 3)
        up_sum = reduce_owners(up_pieces.reshape(owners, cut, hidden))
        down_sum = reduce_owners(down_part.reshape(owners, hidden // owners, width))

    io_got = io_got + after(jnp.int32(0), ff_parts[0]).astype(BF)
    io_full = both(io_got, swap(io_got)).reshape(shards, 2, 2, half, width)
    out_full = io_full[:, :, 0].reshape(width, width)
    in_full = io_full[:, :, 1].reshape(width, width)[:, :3 * cols].T
    out_own = lax.dynamic_slice_in_dim(out_full, group * cols, cols, 0)
    run_at = both_all[:, 2 * tokens, :held].reshape(-1).astype(jnp.int32)
    runs = run_at.shape[0]
    at_run = lax.broadcasted_iota(jnp.int32, (runs, runs), 0)
    of_run = lax.broadcasted_iota(jnp.int32, (runs, runs), 1)
    order = jnp.sum(jnp.where(run_at[None] == at_run, of_run, 0), 1)

    ladder = 10000.0 ** (-jnp.arange(0, ROT, 2, dtype=F32) / ROT)
    angle = jnp.arange(length, dtype=jnp.int32).astype(F32).reshape(tiles, 1, TILE) * ladder[None, :, None]
    cosine, sine = jnp.cos(angle), jnp.sin(angle)

    bias_own = lax.dynamic_index_in_dim(full_in_bias.reshape(3, groups, cols), group, 1, keepdims=False)
    qkv = project(order, both_all, in_full, out_own, bias_own.reshape(-1, 1), gain_one[None], shift_one[None],
                  cosine, sine)
    spots = jnp.concatenate([sharer[None].astype(jnp.int32), order])
    ff_got = at_distance(ff_parts)
    mixed_out, back_qkv = attend(spots, qkv, cosine, sine, owners, sharers)
    up_sum = jnp.concatenate(by_distance(up_sum.reshape(shards, small_step, hidden), after(shard, back_qkv)), 0)
    mixed_own = give_half(mixed_out.reshape(owners // 2, 2, own_heads, held, HEAD, RUN), 1)
    mixed_got = spread_out(mixed_own, "ctx", parity)
    if joined:
        ff_own = jnp.concatenate([up_sum, down_sum], 0)
        ff_all = lax.all_gather(ff_own, "ctx", axis=0, tiled=False)
        up_all, down_all = ff_all[:, :cut], ff_all[:, cut:]
    else:
        ff_own = up_sum
        up_all, down_all = [lax.all_gather(v, "ctx", axis=0, tiled=False) for v in (up_sum, down_sum)]
    x32, grad32 = x.astype(F32), grad.astype(F32)
    gain_row, shift_row = gain_one[None], shift_one[None]
    in_part, out_part, in_bias_part, gain_one_part, shift_one_part = back_to_weight(
        order, back_qkv, in_full, both_all, mixed_out, gain_row, shift_row, (mixed_own, ff_own))
    if packed:
        up_weight_gradient, down_weight_gradient = place_ff(shard[None], ff_all, shards, small_step)
    else:
        up_all = up_all.reshape(owners, shards, small_step, hidden)
        up_all = [lax.dynamic_index_in_dim(up_all, shard ^ f, 1, keepdims=False) for f in range(shards)]
        up_weight_gradient = jnp.concatenate(up_all, -1).reshape(rows, shards * hidden).astype(F32)
        down_weight_gradient = down_all.reshape(hidden, width).astype(F32)

    mixed_got = mixed_got + after(jnp.int32(0), in_part).astype(BF)
    ff_sum = total(ff_got) + after(jnp.int32(0), down_weight_gradient).astype(F32)
    mixed = jnp.sum(mixed_got.astype(F32).reshape(groups, sharers // 2, own_heads, held, HEAD, RUN), 1)
    mixed = mixed.transpose(0, 1, 3, 2, 4).reshape(width, tokens).astype(BF)
    branch = mm(mixed, out_full, (0, 0))
    output = x32 + (branch + full_out_bias) + (ff_sum[:tokens] + full_down_bias)

    in_bias_full = lax.dynamic_update_slice_in_dim(
        jnp.zeros((3, groups, cols), F32), in_bias_part.reshape(3, 1, cols), group, 1)
    lines = [in_bias_full.reshape(-1), jnp.sum(grad32, 0), gain_one_part[0], shift_one_part[0], gain_two_part[0],
             shift_two_part[0]]
    lines = [v.reshape(shards, -1) for v in lines]
    at_shard = (jnp.arange(shards) == shard)[:, None]
    lines.append(jnp.where(at_shard, up_bias_part, 0.0))
    line_sizes = [v.shape[1] for v in lines]
    lines = jnp.concatenate(lines, 1).astype(BF).reshape(shards, 2, -1, width - 3 * cols)
    line_rows = lines.shape[2]
    lines = jnp.pad(lines, ((0, 0), (0, 0), (0, half - line_rows), (0, 0)))
    out_rows = lax.dynamic_update_slice_in_dim(
        jnp.zeros((width, width), BF), out_part.astype(BF), group * cols, 0)
    in_pieces = jnp.concatenate([in_part.reshape(shards, 2, half, 3 * cols), lines], 3)
    pieces = jnp.concatenate([out_rows.reshape(shards, 2, half, width), in_pieces], 2)
    pieces = give_half(pieces, 1, after(core, mixed_got))
    e_runs = back_to_input(order, back_qkv, in_full, gain_row, (pieces, pieces))
    e_sum = lax.psum_scatter(e_runs.reshape(length, width), "ctx", scatter_dimension=0, tiled=True)
    pieces = total(by_distance(pieces, shard)).astype(BF)
    pieces = pieces + after(jnp.int32(0), down_weight_gradient).astype(BF)
    in_weight_gradient, out_weight_gradient, line_sum = place_io(
        core, *gather_owners(pieces), cols)
    line_sum = line_sum.reshape(2, half, -1)[:, :line_rows].reshape(-1)
    totals, at = [], 0
    for size in line_sizes:
        totals.append(line_sum[at:at + size])
        at += size

    e = e_sum.astype(F32) + ff_sum[tokens:]
    xhat, inverse = normalize(x32)
    input_gradient = grad32 + inverse * (
        e - jnp.mean(e, -1, keepdims=True) - xhat * jnp.mean(e * xhat, -1, keepdims=True))
    return (
        output.astype(BF)[None], input_gradient[None], in_weight_gradient, totals[0], out_weight_gradient, totals[1],
        up_weight_gradient, totals[6], down_weight_gradient, totals[1], totals[2], totals[3], totals[4], totals[5],
    )


def solution(mesh):
    token, matrix, vector = P("fsdp", "ctx", None), P("fsdp", None), P("fsdp")
    return jax.shard_map(
        on_device,
        mesh=mesh,
        in_specs=(token, P("fsdp", "ctx"), matrix, vector, matrix, vector, matrix, vector, matrix, vector,
                  vector, vector, vector, vector, token),
        out_specs=(token, token, matrix, vector, matrix, vector, matrix, vector, matrix, vector,
                   vector, vector, vector, vector),
        check_vma=False,
    )
```
